512 devices in a mesh: tensor: 8 (over y_lo, x), expert: 32 (over y_hi, z), dp: 2 (over core).
Axes of the slice: x: 4, y: 4 (y_hi: 2, y_lo: 2; y = y_hi * 2 + y_lo), z: 16, core: 2. Of those that a mesh axis runs over, the one named last changes fastest.
Arguments:
- patches: bfloat16 [64, 64, 4608], P(('dp', 'expert')), parts along dimension 0, may hold values from -700 to 700
- patch_gain: float32 [1152], replicated, may hold values from 0.5 to 1.5
- patch_bias: float32 [1152], replicated, may hold values from -3 to 3
- first_weight: bfloat16 [4608, 2304], P('expert', 'tensor'), may hold values from -0.09375 to 0.09375
- first_bias: float32 [2304], P('tensor'), may hold values from -3 to 3
- second_weight: bfloat16 [4096, 2304], P('expert', 'tensor'), may hold values from -0.125 to 0.125
- second_bias: float32 [4096], replicated, may hold values from -3 to 3
- image_units: int32 [64, 32], P(('dp', 'expert')), parts along dimension 0, may hold values from 1 to 2, as said below
- image_owner: int32 [64, 32], P(('dp', 'expert')), parts along dimension 0, may hold values from 0 to 31, as said below
- image_offset: int32 [64, 32], P(('dp', 'expert')), parts along dimension 0, may hold values from 0 to 127, as said below
- text_states: bfloat16 [64, 128, 4096], P(('dp', 'expert')), parts along dimension 0, may hold values from -700 to 700
- token_gain: float32 [4096], replicated, may hold values from 0.1 to 1.9
- expert_ids: int32 [64, 128, 8], P(('dp', 'expert')), parts along dimension 0, may hold values from 0 to 127, as said below
- route_weights: float32 [64, 128, 8], P(('dp', 'expert')), parts along dimension 0, may hold values from 0.1 to 1
- gate_weight: bfloat16 [32, 4096, 1024], P('expert', None, 'tensor'), may hold values from -0.09375 to 0.09375
- up_weight: bfloat16 [32, 4096, 1024], P('expert', None, 'tensor'), may hold values from -0.09375 to 0.09375
- down_weight: bfloat16 [32, 1024, 4096], P('expert', None, 'tensor'), may hold values from -0.1875 to 0.1875
Outputs:
- mixed: bfloat16 [64, 128, 4096], P(('dp', 'expert'), None, 'tensor'), parts along dimension 0
The draws below stay inside these ranges and needn't reach their ends.
There are 2 independent parts, one for each index of `dp`. The reference program is written for one: setup_inputs(seed, part) draws one part's arguments, and reference() takes and returns one part's arrays. A program takes and returns all parts, laid end to end along the dimension named above; an argument that names none is the same for every part. Nothing has to cross between parts.
Inputs may be any that keep to these rules, and one draw needn't show every extreme that they name: `image_units`: A group's images stand one after another from its first unit. In every draw one owner receives 32 images of 2 tokens each, and one group's images fill all 64 units. `image_owner`: image k of group g goes to owner (g + s_k) mod 32, with 32 different shifts s_k, so a group sends exactly one image to each owner and every owner receives 32 images. `image_offset`: image k lies within positions k * 4 to (k + 1) * 4 - 1 of its owner's sequence, so the images of one owner never share a position. `expert_ids`: each token names 8 different experts; those below 32 are in flight. No expert is named by more than 16 tokens of one owner's sequence, and one expert in flight is named by exactly 16 tokens of every owner's sequence.
All inputs are finite; a program needn't handle non-finite values.
Results may differ from the reference program's by a relative error of at most 0.0082.
Values may be sent and summed in bfloat16 or wider, within the bound.
A program may use at most 64 MiB of HBM per device.

```python
import math
import jax
import jax.numpy as jnp
from jax import lax

D = 4096
DV = 1152
TOP = 8
HM = 2304
HE = 1024
MAXL = 2
SEQ = 128
GROUPS = 32
IMGS = 32
UNITS = 64
ALL = 128
CAP = 16


def image_layout(key):
    key = jax.random.fold_in(key, 101)
    subkeys = jax.random.split(key, 4)
    shifts = jax.random.permutation(subkeys[0], GROUPS)[:IMGS].astype(jnp.int32)
    group_col = jnp.arange(GROUPS, dtype=jnp.int32)[:, None]
    owners = (group_col + shifts[None, :]) % GROUPS
    lowest = max(1, MAXL // 2)
    counts = jax.random.randint(subkeys[1], (GROUPS, IMGS), lowest, MAXL + 1, dtype=jnp.int32)
    chosen = jax.random.randint(subkeys[2], (), 0, GROUPS, dtype=jnp.int32)
    senders = (chosen - shifts) % GROUPS
    counts = counts.at[senders, jnp.arange(IMGS)].set(MAXL)
    counts = counts.at[senders[0], :].set(MAXL)
    region = SEQ // IMGS
    spacing = jax.random.randint(subkeys[3], (GROUPS, IMGS), 0, region - counts + 1, dtype=jnp.int32)
    offsets = jnp.arange(IMGS, dtype=jnp.int32)[None, :] * region + spacing
    return (counts, owners, offsets)


def draw_image_units(key, part):
    return image_layout(key)[0]


def draw_image_owner(key, part):
    return image_layout(key)[1]


def draw_image_offset(key, part):
    return image_layout(key)[2]


def owner_routes(key, target):
    subkeys = jax.random.split(key, 4)
    total = TOP * SEQ
    lengths = jax.random.randint(subkeys[0], (ALL,), CAP // 2, CAP + 1, dtype=jnp.int32).at[0].set(CAP)
    bounds = jnp.cumsum(lengths)
    places = jnp.arange(total, dtype=jnp.int32)
    runs = jnp.sum((bounds[None, :] <= places[:, None]).astype(jnp.int32), axis=1)
    shuffle = jax.random.permutation(subkeys[1], ALL).astype(jnp.int32)
    labels = (shuffle[runs] + target - shuffle[0]) % ALL
    table = labels.reshape(TOP, SEQ).T
    order = jax.random.permutation(subkeys[2], SEQ)
    table = table[order]
    turns = jax.random.randint(subkeys[3], (SEQ, 1), 0, TOP, dtype=jnp.int32)
    column = (jnp.arange(TOP, dtype=jnp.int32)[None, :] + turns) % TOP
    return jnp.take_along_axis(table, column, axis=1)


def draw_expert_ids(key, part):
    key = jax.random.fold_in(key, 202)
    first_key, second_key = jax.random.split(key)
    target = jax.random.randint(first_key, (), 0, GROUPS, dtype=jnp.int32)
    owner_keys = jax.random.split(second_key, GROUPS)
    return jax.vmap(lambda one_key: owner_routes(one_key, target))(owner_keys)


def draw_patches(key, part):
    key = jax.random.fold_in(key, 7)
    subkeys = jax.random.split(key, 3)
    row_scale = jnp.exp(jax.random.uniform(subkeys[1], (GROUPS, UNITS, 4, 1), minval=0.0, maxval=2.3))
    col_scale = jnp.exp(jax.random.uniform(subkeys[2], (DV,), minval=0.0, maxval=2.3))
    values = jnp.clip(jax.random.normal(subkeys[0], (GROUPS, UNITS, 4, DV)), -5.0, 5.0)
    return (values * row_scale * col_scale).reshape(GROUPS, UNITS, 4 * DV).astype(jnp.bfloat16)


def draw_text_states(key, part):
    key = jax.random.fold_in(key, 5)
    subkeys = jax.random.split(key, 3)
    row_scale = jnp.exp(jax.random.uniform(subkeys[1], (GROUPS, SEQ, 1), minval=0.0, maxval=2.3))
    col_scale = jnp.exp(jax.random.uniform(subkeys[2], (D,), minval=0.0, maxval=2.3))
    values = jnp.clip(jax.random.normal(subkeys[0], (GROUPS, SEQ, D)), -5.0, 5.0)
    return (values * row_scale * col_scale).astype(jnp.bfloat16)


def block_levels(own_key, extent, shards, low, top_value):
    loudness = 1.0
    for axis_at, parts in shards:
        heights = jax.random.uniform(jax.random.fold_in(jax.random.fold_in(own_key, 6), axis_at), (parts,), jnp.float32, low / len(shards), top_value / len(shards))
        loudness = loudness * jnp.repeat(jnp.exp(heights), extent[axis_at] // parts).reshape((-1,) + (1,) * (len(extent) - 1 - axis_at))
    return loudness


def scatter_about(key, shape, scale, bound, cuts=(), kind=jnp.bfloat16):
    values = jax.random.normal(key, shape, jnp.float32) * scale
    if len(cuts) > 0:
        values = block_levels(key, shape, cuts, -0.22, 0.18) * values
    return jnp.clip(values, min=-bound, max=bound).astype(kind)


def setup_inputs(seed: int = 0, part: int = 0) -> dict:
    seeds = jax.random.split(jax.random.key(seed), 18)
    part_splits = jax.random.split(jax.random.fold_in(seeds[17], part), 18)
    patches = draw_patches(jax.random.fold_in(jax.random.fold_in(seeds[17], part), 71), part)
    patch_gain = jnp.clip(1.0 + 0.1 * jax.random.normal(seeds[1], (DV,), jnp.float32), 0.5, 1.5)
    patch_bias = scatter_about(seeds[2], (DV,), 0.5, 3.0, (), jnp.float32)
    first_weight = scatter_about(seeds[3], (4 * DV, HM), (4 * DV) ** -0.5, 0.09375, ((0, 32), (1, 8)))
    first_bias = scatter_about(seeds[4], (HM,), 0.5, 3.0, ((0, 8),), jnp.float32)
    second_weight = scatter_about(seeds[5], (D, HM), HM ** -0.5, 0.125, ((0, 32), (1, 8)))
    second_bias = scatter_about(seeds[6], (D,), 0.5, 3.0, (), jnp.float32)
    image_units = draw_image_units(jax.random.fold_in(jax.random.fold_in(seeds[17], part), 71), part)
    image_owner = draw_image_owner(jax.random.fold_in(jax.random.fold_in(seeds[17], part), 71), part)
    image_offset = draw_image_offset(jax.random.fold_in(jax.random.fold_in(seeds[17], part), 71), part)
    text_states = draw_text_states(jax.random.fold_in(jax.random.fold_in(seeds[17], part), 71), part)
    token_gain = jnp.clip(1.0 + 0.18 * jax.random.normal(seeds[11], (D,), jnp.float32), 0.1, 1.9)
    expert_ids = draw_expert_ids(jax.random.fold_in(jax.random.fold_in(seeds[17], part), 71), part)
    route_weights = jnp.clip(jnp.exp(math.log(1.0) - 2.3025851 * jax.random.uniform(part_splits[13], (GROUPS, SEQ, TOP), jnp.float32) ** block_levels(part_splits[13], (GROUPS, SEQ, TOP), ((0, 32),), -0.2, 0.2)), 0.1, 1.0)
    gate_weight = scatter_about(seeds[14], (GROUPS, D, HE), D ** -0.5, 0.09375, ((0, 32), (2, 8)))
    up_weight = scatter_about(seeds[15], (GROUPS, D, HE), D ** -0.5, 0.09375, ((0, 32), (2, 8)))
    down_weight = scatter_about(seeds[16], (GROUPS, HE, D), HE ** -0.5, 0.1875, ((0, 32), (2, 8)))
    return dict(patches=patches, patch_gain=patch_gain, patch_bias=patch_bias, first_weight=first_weight, first_bias=first_bias, second_weight=second_weight, second_bias=second_bias, image_units=image_units, image_owner=image_owner, image_offset=image_offset, text_states=text_states, token_gain=token_gain, expert_ids=expert_ids, route_weights=route_weights, gate_weight=gate_weight, up_weight=up_weight, down_weight=down_weight)


def normalize_patches(patches, patch_gain, patch_bias):
    values = patches.astype(jnp.float32).reshape(GROUPS, UNITS, 4, DV)
    center = values - lax.optimization_barrier(jnp.mean(values, axis=-1, keepdims=True))
    variance = lax.optimization_barrier(jnp.mean(center * center, axis=-1, keepdims=True))
    scaled = center * lax.rsqrt(variance + 1e-06) * patch_gain + patch_bias
    return scaled.astype(jnp.bfloat16).reshape(GROUPS * UNITS, 4 * DV)

def reference(patches, patch_gain, patch_bias, first_weight, first_bias, second_weight, second_bias, image_units, image_owner, image_offset, text_states, token_gain, expert_ids, route_weights, gate_weight, up_weight, down_weight):
    unit_rows = normalize_patches(patches, patch_gain, patch_bias)
    first_out = jnp.dot(unit_rows, first_weight, preferred_element_type=jnp.float32) + first_bias
    merger_hidden = jax.nn.gelu(first_out, approximate=False).astype(jnp.bfloat16)
    second_out = lax.dot_general(merger_hidden, second_weight, (((1,), (1,)), ((), ())), preferred_element_type=jnp.float32)
    embedded = (second_out + second_bias).astype(jnp.bfloat16)
    starts = jnp.cumsum(image_units, axis=1) - image_units
    unit_index = jnp.arange(UNITS, dtype=jnp.int32)[None, :]
    target = jnp.full((GROUPS, UNITS), GROUPS * SEQ, jnp.int32)
    for number in range(IMGS):
        begin = starts[:, number:number + 1]
        inside = (unit_index >= begin) & (unit_index < begin + image_units[:, number:number + 1])
        place = image_owner[:, number:number + 1] * SEQ + image_offset[:, number:number + 1] + unit_index - begin
        target = jnp.where(inside, place.astype(jnp.int32), target)
    states = text_states.reshape(GROUPS * SEQ, D).at[target.reshape(-1)].set(embedded, mode='drop')
    widened = states.astype(jnp.float32)
    inverse = lax.rsqrt(lax.optimization_barrier(jnp.mean(widened * widened, axis=1, keepdims=True)) + 1e-06)
    normed = (widened * inverse * token_gain).astype(jnp.bfloat16)
    routes = expert_ids.reshape(GROUPS * SEQ, TOP)
    shares = route_weights.reshape(GROUPS * SEQ, TOP)
    tokens = jnp.arange(GROUPS * SEQ, dtype=jnp.int32)
    slot_total = GROUPS * CAP

    def one_expert(total, inputs):
        gate_matrix, up_matrix, down_matrix, expert = inputs
        chosen = routes == expert
        member = jnp.any(chosen, axis=1).astype(jnp.int32)
        weight = lax.optimization_barrier(jnp.sum(jnp.where(chosen, shares, 0.0), axis=1))
        rank = jnp.cumsum(member) - member
        index = jnp.zeros((slot_total,), jnp.int32).at[jnp.where(member > 0, rank, slot_total)].set(tokens, mode='drop')
        valid = jnp.arange(slot_total, dtype=jnp.int32) < jnp.sum(member)
        picked = normed[index]
        gate_proj = jnp.dot(picked, gate_matrix, preferred_element_type=jnp.float32)
        up_proj = jnp.dot(picked, up_matrix, preferred_element_type=jnp.float32)
        activation = (jax.nn.silu(gate_proj) * up_proj).astype(jnp.bfloat16)
        expert_out = jnp.dot(activation, down_matrix, preferred_element_type=jnp.float32).astype(jnp.bfloat16)
        factor = jnp.where(valid, weight[index], 0.0)
        total = total.at[index].add(expert_out.astype(jnp.float32) * factor[:, None])
        return (total, None)
    start_total = jnp.zeros((GROUPS * SEQ, D), jnp.float32)
    total, _ = lax.scan(one_expert, start_total, (gate_weight, up_weight, down_weight, jnp.arange(GROUPS, dtype=jnp.int32)))
    return total.astype(jnp.bfloat16).reshape(GROUPS, SEQ, D)
```

```python
import jax
import jax.numpy as jnp
from jax import lax
from jax.experimental import pallas as pl
from jax.experimental.pallas import tpu as pltpu
from jax.sharding import PartitionSpec as P

BF = jnp.bfloat16
F32 = jnp.float32
I32 = jnp.int32
MESH = pl.DeviceIdType.MESH

PLANES = 16
CHUNKS = 4
PER = PLANES // CHUNKS
ROWS = PER * 32


def offset_of(place):
    if place == 0:
        return 0
    return (place + 1) // 2 if place % 2 else PLANES - place // 2


def nn(a, b):
    return jnp.dot(a, b, preferred_element_type=F32)


def nt(a, b):
    return lax.dot_general(a, b, (((1,), (1,)), ((), ())), preferred_element_type=F32)


def tn(a, b):
    return lax.dot_general(a, b, (((0,), (0,)), ((), ())), preferred_element_type=F32)


def wait(ref, sem):
    pltpu.make_async_copy(ref, ref, sem).wait()


def kernel(
    patches, pgain, pbias, w1, b1, w2, b2, units, owners, offsets, text, tgain,
    ids, shares, gate, up, down,
    out,
    g1, g2, pv, xn, b1p, hid, p1s, p1r, p2s, p2r, sel_own, sel_far, info_s, info_r,
    img_s, img_r, tx, rt, wt, pick, st, xs, xr, xk, wgu, dw, gx, ps, pr, ss_s, ss_r,
    act_s, act_r, ob, rb,
    s_w, r_w, s_c, r_c, l_sem, s_gu, r_gu, s_one, r_one, s_info, r_info, s_p2, r_p2,
    s_img, r_img, s_disp, r_disp, s_ag, r_ag, s_rs, r_rs, s_ss, r_ss, s_act, r_act,
    s_ret, r_ret,
):
    e = lax.axis_index("expert")
    t = lax.axis_index("tensor")
    core = lax.axis_index("dp")
    yh, z = e // 16, e % 16
    yl, x = t // 4, t % 4
    y = 2 * yh + yl
    far = (1 - yh) * 16 + z
    col = yh * 2048 + x * 512 + yl * 256
    far_col = (1 - yh) * 2048 + x * 512 + yl * 256

    def send(src, dst, ssem, rsem, **dev):
        copy = pltpu.make_async_remote_copy(
            src_ref=src, dst_ref=dst, send_sem=ssem, recv_sem=rsem,
            device_id=dev, device_id_type=MESH,
        )
        copy.start()
        return copy

    local = [
        (patches.at[0, :, pl.ds(pl.multiple_of(2304 * yh, 128), 2304)], pv.at[yh]),
        (text.at[0, :, pl.ds(pl.multiple_of(col, 128), 256)], tx.at[yh]),
        (down.at[0], dw),
    ]
    for h in range(2):
        rows = pl.ds(pl.multiple_of(2048 * h + 512 * x, 512), 512)
        local.append((gate.at[0, rows, :], wgu.at[x, pl.ds(512 * h, 512), pl.ds(0, 128)]))
        local.append((up.at[0, rows, :], wgu.at[x, pl.ds(512 * h, 512), pl.ds(128, 128)]))
    local = [pltpu.make_async_copy(a, b, l_sem.at[i]) for i, (a, b) in enumerate(local)]
    for copy in local:
        copy.start()

    barrier = pltpu.get_barrier_semaphore()

    def greet(**dev):
        pl.semaphore_signal(barrier, inc=1, device_id=dev, device_id_type=MESH)

    for i in range(1, 32):
        greet(expert=lax.rem(e + i, 32))
    for i in range(1, 8):
        greet(tensor=lax.rem(t + i, 8))
    greet(dp=1 - core)
    greet(expert=far, tensor=lax.rem(t + 4, 8))

    g1[z, :, 256:] = jnp.zeros((144, 128), BF)
    g2[z, :, 256:] = jnp.zeros((128, 128), BF)
    g1[z, :, :288] = w1[...]
    g2[z, :, :288] = w2[...]
    b1p[...] = jnp.zeros((1, 384), F32)
    b1p[:, :288] = b1[...]

    pl.semaphore_wait(barrier, 40)

    step_z = 1 - 2 * core
    nxt = yh * 16 + lax.rem(z + step_z + 16, 16)
    sends = []
    gathered = (g1, g2)
    for w, g in enumerate(gathered):
        sends.append(send(g.at[z], g.at[z], s_w.at[w, 0], r_w.at[w, 0], expert=nxt))
    far_half = pl.ds(pl.multiple_of(2304 * (1 - yh), 128), 2304)
    sends.append(send(patches.at[0, :, far_half], pv.at[yh], s_one.at[0], r_one.at[0], expert=far))
    far_cols = pl.ds(pl.multiple_of(far_col, 128), 256)
    sends.append(send(text.at[0, :, far_cols], tx.at[yh], s_one.at[1], r_one.at[1], expert=far))
    for i in range(1, 4):
        xx = lax.rem(x + i, 4)
        for h in range(2):
            rows = pl.ds(pl.multiple_of(2048 * h + 512 * xx, 512), 512)
            for k, source in enumerate((gate, up)):
                send(
                    source.at[0, rows, :],
                    wgu.at[x, pl.ds(512 * h, 512), pl.ds(128 * k, 128)],
                    s_gu, r_gu, tensor=yl * 4 + xx,
                )

    def iota(shape, dim):
        return lax.broadcasted_iota(I32, shape, dim)

    def route():
        lane = iota((128, 128), 1)
        place = lane >> 1
        dist = jnp.where((place & 1) == 1, (place + 1) >> 1, (16 - (place >> 1)) & 15)
        expert = jnp.where(lane < 32, (lane & 1) * 16 + ((z + dist) & 15), -1)
        member = jnp.zeros((128, 128), F32)
        share = jnp.zeros((128, 128), F32)
        for k in range(8):
            named = ids[:, k : k + 1] == expert
            member = jnp.where(named, 1.0, member)
            share = share + jnp.where(named, shares[:, k : k + 1], 0.0)
        before = (iota((128, 128), 1) < iota((128, 128), 0)).astype(F32).astype(BF)
        rank = nn(before, member.astype(BF))
        rt[yh] = jnp.where(member > 0.5, rank, -1.0).T[:32].astype(BF)
        wt[...] = share.T[:32]
        sends.append(send(rt.at[yh], rt.at[yh], s_one.at[2], r_one.at[2], expert=far))

    def images():
        unit_row = units[...].astype(F32)
        first = (iota((32, 32), 0) < iota((32, 32), 1)).astype(F32).astype(BF)
        starts = nn(jnp.broadcast_to(unit_row, (8, 32)).astype(BF), first)[:1]
        slot = iota((128, 32), 0)
        owner = ((slot >> 1) & 1) * 16 + ((z + (slot >> 3)) & 15)
        match = (owners[...] == owner) & (((slot >> 2) & 1) == yh)

        def pick_out(row):
            return jnp.sum(jnp.where(match, row, 0.0), axis=1, keepdims=True)

        start, count = pick_out(starts), pick_out(unit_row)
        offset = pick_out(offsets[...].astype(F32))
        column = iota((128, 1), 0)
        turn = (column & 1).astype(F32)
        valid = turn < count
        base = (yh * 64).astype(F32)
        source = jnp.where(valid, base + start + turn, -1.0)
        position = jnp.where(valid, ((column >> 1) & 1).astype(F32) * 128.0 + offset + turn, -1.0)
        sel_own[...] = (iota((128, 128), 1).astype(F32) == source).astype(F32).astype(BF)
        info_s[...] = jnp.broadcast_to(position, (128, 128)).reshape(16, 8, 128)
        info_r[yh * 16] = info_s[0]
        sends.append(send(sel_own, sel_far, s_one.at[3], r_one.at[3], expert=far))
        for d in range(16):
            zz = lax.rem(z + d, 16)
            dst = info_r.at[yh * 16 + d]
            send(info_s.at[d], dst, s_info, r_info, expert=(1 - yh) * 16 + zz)
            if d > 0:
                send(info_s.at[d], dst, s_info, r_info, expert=yh * 16 + zz)

    def norm_patches(own):
        g = yh if own else 1 - yh
        if own:
            local[0].wait()
        else:
            wait(pv.at[g], r_one.at[0])
        for p in range(2):
            part = pl.ds(1152 * p, 1152)
            v = pv[g, :, part].astype(F32)
            center = v - jnp.mean(v, axis=1, keepdims=True)
            variance = jnp.mean(center * center, axis=1, keepdims=True)
            scaled = center * lax.rsqrt(variance + 1e-06) * pgain[...] + pbias[...]
            xn[g, :, part] = scaled.astype(BF)

    def selections():
        wait(rt.at[1 - yh], r_one.at[2])
        for oy in range(2):
            ranks = rt[oy].astype(F32).reshape(32, 1, 128)
            slots = iota((32, 16, 128), 1).astype(F32)
            pick[oy] = (ranks == slots).astype(F32).reshape(512, 128).astype(BF)

    jobs = {
        0: [route, images],
        1: [lambda: norm_patches(True)],
        2: [lambda: norm_patches(False)],
        3: [selections],
    }
    for s in range(8):
        origin = lax.rem(z - step_z * (s + 1) + 32, 16)
        for w, g in enumerate(gathered):
            wait(g.at[origin], r_w.at[w, s])
            if s < 7:
                block = g.at[origin]
                sends.append(send(block, block, s_w.at[w, s + 1], r_w.at[w, s + 1], expert=nxt))
                sends.append(send(block, block, s_c.at[w, s], r_c.at[w, s], dp=1 - core))
        for job in jobs.get(s, ()):
            job()

    def other_core(w):
        for s in range(7):
            origin = lax.rem(z + step_z * (s + 1) + 32, 16)
            wait(gathered[w].at[origin], r_c.at[w, s])

    other_core(0)
    part1 = nn(xn[...].reshape(128, 2304), g1[...].reshape(2304, 384))
    p1s[...] = part1.astype(BF)
    sends.append(send(p1s, p1r, s_one.at[4], r_one.at[4], expert=far))
    other_core(1)
    wait(p1r, r_one.at[4])
    v = part1 + p1r[...].astype(F32) + b1p[...]
    hid[...] = (0.5 * v * (1.0 + lax.erf(v * (0.5**0.5)))).astype(BF)

    def second(tt):
        k = 2 * lax.rem(tt, 4) + tt // 4
        return nt(hid[...], g2[pl.ds(2 * k, 2)].reshape(256, 384))

    for i in range(1, 8):
        tt = lax.rem(t + i, 8)
        p2s[i - 1] = second(tt).astype(BF)
        send(p2s.at[i - 1], p2r.at[i - 1], s_p2, r_p2, tensor=tt)
    total = second(t) + b2[:, pl.ds(pl.multiple_of(col, 128), 256)]
    wait(info_r.at[pl.ds(0, 31)], r_info)
    wait(sel_far, r_one.at[3])
    chosen = sel_own[...] + sel_far[...]
    wait(p2r.at[pl.ds(0, 7)], r_p2)
    for i in range(7):
        total = total + p2r[i].astype(F32)
    emb = total.astype(BF)

    rows = nn(chosen, emb).reshape(16, 8, 256)
    img_s[...] = jnp.concatenate([rows[:, :, :128], rows[:, :, 128:]], axis=1).astype(BF)
    img_r[0] = img_s[0]
    for d in range(1, 16):
        send(img_s.at[d], img_r.at[d], s_img, r_img, expert=yh * 16 + lax.rem(z + d, 16))

    local[1].wait()
    wait(tx.at[1 - yh], r_one.at[1])
    position = jnp.maximum(info_r[pl.ds(0, 16)], info_r[pl.ds(16, 16)])
    blank = jnp.zeros((16, 8, 128), F32)
    placed = []
    for oy in range(2):
        hit = (position == (iota((16, 8, 128), 2) + oy * 128).astype(F32)).astype(F32)
        low = jnp.concatenate([hit, blank], axis=1).reshape(256, 128).astype(BF)
        high = jnp.concatenate([blank, hit], axis=1).reshape(256, 128).astype(BF)
        covered = tn(low, jnp.ones((256, 128), BF)) > 0.5
        placed.append((low, high, covered))
    wait(img_r.at[pl.ds(0, 15)], r_img)
    arrived = img_r[...].reshape(256, 128)
    for oy in range(2):
        low, high, covered = placed[oy]
        for half, hits in enumerate((low, high)):
            part = pl.ds(128 * half, 128)
            base = tx[oy, :, part].astype(F32)
            st[oy, :, part] = jnp.where(covered, tn(hits, arrived), base).astype(BF)

    for oy in range(2):
        xs[:, :, 16 * oy : 16 * oy + 16, :] = nn(pick[oy], st[oy]).astype(BF).reshape(16, 2, 16, 256)
    for p in range(1, 16):
        send(xs.at[p], xr.at[p], s_disp, r_disp.at[p], expert=yh * 16 + lax.rem(z + offset_of(p), 16))

    def forward(c):
        for p in range(PER * c, PER * c + PER):
            if p > 0:
                wait(xr.at[p], r_disp.at[p])
            block = xs.at[p] if p == 0 else xr.at[p]
            xk[p, y] = block[yh]
            dst = xk.at[p, y]
            send(block.at[yh], dst, s_ag, r_ag.at[c], tensor=lax.rem(t + 4, 8))
            send(block.at[1 - yh], dst, s_ag, r_ag.at[c], expert=far)
            send(block.at[1 - yh], dst, s_ag, r_ag.at[c], expert=far, tensor=lax.rem(t + 4, 8))

    def project(c):
        wait(xk.at[pl.ds(PER * c, 3)], r_ag.at[c])
        if c == 0:
            for copy in local[3:]:
                copy.wait()
            wait(wgu.at[pl.ds(0, 3)], r_gu)
        squares = jnp.zeros((8, ROWS), F32)
        ones = jnp.ones((8, 256), BF)
        for yy in range(4):
            v = xk[PER * c : PER * c + PER, yy].reshape(ROWS, 256).astype(F32)
            start = 2048 * (yy // 2) + 256 * (yy % 2) + 512 * x
            gain = tgain[:, pl.ds(pl.multiple_of(start, 128), 256)]
            gx[:, 256 * yy : 256 * yy + 256] = (v * gain).astype(BF)
            square = v * v
            high = square.astype(BF)
            low = (square - high.astype(F32)).astype(BF)
            squares = squares + nt(ones, high) + nt(ones, low)
        ss_s[c] = squares
        for i in range(1, 4):
            xx = lax.rem(x + i, 4)
            send(ss_s.at[c], ss_r.at[c, i - 1], s_ss, r_ss.at[c], tensor=yl * 4 + xx)
            ps[c, i] = nn(gx[...], wgu[xx]).astype(BF)
            send(ps.at[c, i], pr.at[c, i - 1], s_rs, r_rs.at[c], tensor=yl * 4 + xx)
        ps[c, 0] = nn(gx[...], wgu[x]).astype(BF)

    def activate(c):
        wait(ss_r.at[c], r_ss.at[c])
        wait(pr.at[c], r_rs.at[c])
        squares = ss_s[c, 0:1] + ss_r[c, 0, 0:1] + ss_r[c, 1, 0:1] + ss_r[c, 2, 0:1]
        inverse = lax.rsqrt(squares * (1.0 / 4096.0) + 1e-06)
        eye = iota((ROWS, ROWS), 0) == iota((ROWS, ROWS), 1)
        inverse = jnp.sum(jnp.where(eye, inverse, 0.0), axis=1, keepdims=True)
        sums = ps[c, 0].astype(F32) + pr[c, 0].astype(F32) + pr[c, 1].astype(F32) + pr[c, 2].astype(F32)
        sums = sums * inverse
        gated, upped = sums[:, :128], sums[:, 128:]
        activation = (gated / (1.0 + jnp.exp(-gated)) * upped).astype(BF)
        act_s[c] = activation
        mine = pl.ds(pl.multiple_of(t * 128, 128), 128)
        act_r[c, :, mine] = activation
        for i in range(1, 8):
            send(act_s.at[c], act_r.at[c, :, mine], s_act, r_act.at[c], tensor=lax.rem(t + i, 8))

    def produce(c):
        if c == 0:
            local[2].wait()
        wait(act_r.at[c, :, pl.ds(0, 896)], r_act.at[c])
        ob[PER * c : PER * c + PER] = nn(act_r[c], dw[...]).astype(BF).reshape(PER, 2, 16, 512)
        for p in range(PER * c, PER * c + PER):
            zz = lax.rem(z - offset_of(p) + 16, 16)
            dst = rb.at[2 * p + yh]
            if p == 0:
                rb[yh] = ob[0, yh]
                send(ob.at[0, 1 - yh], dst, s_ret, r_ret, expert=far)
            else:
                for oy in range(2):
                    send(ob.at[p, oy], dst, s_ret, r_ret, expert=oy * 16 + zz)

    for turn in range(CHUNKS + 4):
        if turn < CHUNKS:
            forward(turn)
        if 0 <= turn - 1 < CHUNKS:
            project(turn - 1)
        if 0 <= turn - 2 < CHUNKS:
            activate(turn - 2)
        if 0 <= turn - 3 < CHUNKS:
            produce(turn - 3)

    weight = pick[yh].astype(F32).reshape(32, 16, 128) * wt[...].reshape(32, 1, 128)
    weight = weight.reshape(512, 128)
    high = weight.astype(BF)
    low = (weight - high.astype(F32)).astype(BF)
    wait(rb.at[pl.ds(0, 31)], r_ret)
    back = rb[...].reshape(512, 512)
    out[0] = (tn(high, back) + tn(low, back)).astype(BF)

    for copy in sends:
        copy.wait_send()
    wait(wgu.at[pl.ds(0, 3)], s_gu)
    wait(info_r.at[pl.ds(0, 31)], s_info)
    wait(p2r.at[pl.ds(0, 7)], s_p2)
    wait(img_r.at[pl.ds(0, 15)], s_img)
    wait(xr.at[pl.ds(0, 15)], s_disp)
    wait(xk.at[pl.ds(0, 12)], s_ag)
    wait(pr, s_rs)
    wait(ss_r, s_ss)
    wait(act_r.at[:, :, pl.ds(0, 896)], s_act)
    wait(rb.at[pl.ds(0, 31)], s_ret)


def body(
    patches, patch_gain, patch_bias, first_weight, first_bias, second_weight, second_bias,
    image_units, image_owner, image_offset, text_states, token_gain, expert_ids,
    route_weights, gate_weight, up_weight, down_weight,
):
    vmem = pl.BlockSpec(memory_space=pltpu.VMEM)
    anywhere = pl.BlockSpec(memory_space=pl.ANY)
    dma = pltpu.SemaphoreType.DMA
    scratch = [
        pltpu.VMEM((16, 144, 384), BF),
        pltpu.VMEM((16, 128, 384), BF),
        pltpu.VMEM((2, 64, 2304), BF),
        pltpu.VMEM((2, 64, 2304), BF),
        pltpu.VMEM((1, 384), F32),
        pltpu.VMEM((128, 384), BF),
        pltpu.VMEM((128, 384), BF),
        pltpu.VMEM((128, 384), BF),
        pltpu.VMEM((7, 128, 256), BF),
        pltpu.VMEM((7, 128, 256), BF),
        pltpu.VMEM((128, 128), BF),
        pltpu.VMEM((128, 128), BF),
        pltpu.VMEM((16, 8, 128), F32),
        pltpu.VMEM((32, 8, 128), F32),
        pltpu.VMEM((16, 16, 128), BF),
        pltpu.VMEM((16, 16, 128), BF),
        pltpu.VMEM((2, 128, 256), BF),
        pltpu.VMEM((2, 32, 128), BF),
        pltpu.VMEM((32, 128), F32),
        pltpu.VMEM((2, 512, 128), BF),
        pltpu.VMEM((2, 128, 256), BF),
        pltpu.VMEM((16, 2, 32, 256), BF),
        pltpu.VMEM((16, 2, 32, 256), BF),
        pltpu.VMEM((16, 4, 32, 256), BF),
        pltpu.VMEM((4, 1024, 256), BF),
        pltpu.VMEM((1024, 512), BF),
        pltpu.VMEM((ROWS, 1024), BF),
        pltpu.VMEM((CHUNKS, 4, ROWS, 256), BF),
        pltpu.VMEM((CHUNKS, 3, ROWS, 256), BF),
        pltpu.VMEM((CHUNKS, 8, ROWS), F32),
        pltpu.VMEM((CHUNKS, 3, 8, ROWS), F32),
        pltpu.VMEM((CHUNKS, ROWS, 128), BF),
        pltpu.VMEM((CHUNKS, ROWS, 1024), BF),
        pltpu.VMEM((16, 2, 16, 512), BF),
        pltpu.VMEM((32, 16, 512), BF),
        dma((2, 8)), dma((2, 8)), dma((2, 7)), dma((2, 7)),
        dma((7,)), dma, dma, dma((5,)), dma((5,)),
        dma, dma, dma, dma, dma, dma,
        dma, dma((16,)), dma, dma((CHUNKS,)),
        dma, dma((CHUNKS,)), dma, dma((CHUNKS,)), dma, dma((CHUNKS,)),
        dma, dma,
    ]
    call = pl.pallas_call(
        kernel,
        out_shape=jax.ShapeDtypeStruct((1, 128, 512), BF),
        in_specs=[
            anywhere, vmem, vmem, vmem, vmem, vmem, vmem, vmem, vmem, vmem, anywhere, vmem,
            vmem, vmem, anywhere, anywhere, anywhere,
        ],
        out_specs=vmem,
        scratch_shapes=scratch,
        compiler_params=pltpu.CompilerParams(
            collective_id=0, has_side_effects=True, vmem_limit_bytes=48 * 1024 * 1024
        ),
    )
    return call(
        patches, patch_gain[None], patch_bias[None], first_weight, first_bias[None],
        second_weight, second_bias[None], image_units, image_owner, image_offset,
        text_states, token_gain[None], expert_ids[0], route_weights[0],
        gate_weight, up_weight, down_weight,
    )


def solution(mesh):
    in_specs = (
        P(("dp", "expert"), None, None),
        P(),
        P(),
        P("expert", "tensor"),
        P("tensor"),
        P("expert", "tensor"),
        P(),
        P(("dp", "expert"), None),
        P(("dp", "expert"), None),
        P(("dp", "expert"), None),
        P(("dp", "expert"), None, None),
        P(),
        P(("dp", "expert"), None, None),
        P(("dp", "expert"), None, None),
        P("expert", None, "tensor"),
        P("expert", None, "tensor"),
        P("expert", None, "tensor"),
    )
    out_specs = P(("dp", "expert"), None, "tensor")
    return jax.shard_map(body, mesh=mesh, in_specs=in_specs, out_specs=out_specs, check_vma=False)
```

```python
import jax
import jax.numpy as jnp
from jax import lax
from jax.experimental import pallas as pl
from jax.experimental.pallas import tpu as pltpu
from jax.sharding import PartitionSpec as P

BF = jnp.bfloat16
F32 = jnp.float32
I32 = jnp.int32
MESH = pl.DeviceIdType.MESH

PLANES = 16
CHUNKS = 4
PER = PLANES // CHUNKS
ROWS = PER * 32


DISTANCES = (5, 11, 4, 12, 6, 10, 3, 13, 7, 9, 2, 14, 8, 1, 15, 0)
HERE = DISTANCES.index(0)


def nn(a, b):
    return jnp.dot(a, b, preferred_element_type=F32)


def nt(a, b):
    return lax.dot_general(a, b, (((1,), (1,)), ((), ())), preferred_element_type=F32)


def tn(a, b):
    return lax.dot_general(a, b, (((0,), (0,)), ((), ())), preferred_element_type=F32)


def wait(ref, sem):
    pltpu.make_async_copy(ref, ref, sem).wait()


def kernel(
    patches, pgain, pbias, w1, b1, w2, b2, units, owners, offsets, text, tgain,
    ids, shares, gate, up, down,
    out,
    g1, g2, w1x, pv, xn, hid, p1s, p1r, p2s, p2r, sel_own, sel_far, info_own, info_far, info_s, info_r,
    img_s, img_r, tx, rt, wt, pick, st, xs, xr, xk, wgu, dw, gx, ps, pr, ss_s, ss_r,
    act_s, act_r, ob, rb,
    s_w, r_w, s_c, r_c, l_sem, s_gu, r_gu, s_one, r_one, s_info, r_info, s_p2, r_p2,
    s_img, r_img, s_disp, r_disp, s_ag, r_ag, s_rs, r_rs, s_ss, r_ss, s_act, r_act,
    s_ret, r_ret,
):
    e = lax.axis_index("expert")
    t = lax.axis_index("tensor")
    core = lax.axis_index("dp")
    yh, z = e // 16, e % 16
    yl, x = t // 4, t % 4
    y = 2 * yh + yl
    far = (1 - yh) * 16 + z
    col = yh * 2048 + x * 512 + yl * 256

    def send(src, dst, ssem, rsem, **dev):
        copy = pltpu.make_async_remote_copy(
            src_ref=src, dst_ref=dst, send_sem=ssem, recv_sem=rsem,
            device_id=dev, device_id_type=MESH,
        )
        copy.start()
        return copy

    local = [
        (patches.at[0, :, pl.ds(pl.multiple_of(2304 * yh, 128), 2304)], pv.at[yh]),
        (text.at[0, :, pl.ds(pl.multiple_of(col, 128), 256)], tx.at[yh]),
        (down.at[0], dw),
    ]
    for h in range(2):
        rows = pl.ds(pl.multiple_of(2048 * h + 512 * x, 512), 512)
        local.append((gate.at[0, rows, :], wgu.at[x, pl.ds(512 * h, 512), pl.ds(0, 128)]))
        local.append((up.at[0, rows, :], wgu.at[x, pl.ds(512 * h, 512), pl.ds(128, 128)]))
    local = [pltpu.make_async_copy(a, b, l_sem.at[i]) for i, (a, b) in enumerate(local)]
    for copy in local:
        copy.start()

    barrier = pltpu.get_barrier_semaphore()
    after = yh * 16 + lax.rem(z + 1, 16)
    ahead = yh * 16 + lax.rem(z + 15, 16)
    across = lax.rem(t + 4, 8)

    def greet(**dev):
        pl.semaphore_signal(barrier, inc=1, device_id=dev, device_id_type=MESH)

    greet(expert=after)
    greet(expert=ahead)
    greet(dp=1 - core)
    for i in range(1, 8):
        greet(tensor=lax.rem(t + i, 8))
    greet(expert=far)
    greet(expert=far, tensor=across)

    g1[z, :144, :] = w1[:, :256]
    for r in range(9):
        low = 144 if r < 8 else 160
        g1[z, low : low + 16, 32 * (r % 8) : 32 * (r % 8) + 32] = w1[16 * r : 16 * r + 16, 256:288]
    g2[z] = w2[...]

    pl.semaphore_wait(barrier, 12)

    sends, drains = [], []

    def finish():
        for copy in sends:
            copy.wait_send()
        for ref, sem in drains:
            wait(ref, sem)

        @pl.when(core == 1)
        def _():
            for w, g in enumerate(gathered):
                wait(g.at[pl.ds(0, 15)], s_w.at[w])
                wait(g.at[pl.ds(0, 15)], s_c.at[w])

    gathered = (g1, g2)

    def ring(step):
        if step >= 0:
            for w, g in enumerate(gathered):
                for way, to in enumerate((after, ahead)):
                    if step == 7 and way == 1:
                        continue
                    origin = lax.rem(z + (15 - step if way == 0 else step + 1), 16)
                    block = g.at[origin]
                    wait(block, r_w.at[w, way, step])
                    if step < 7 - way:
                        send(block, block, s_w.at[w], r_w.at[w, way, step + 1], expert=to)
                    send(block, block, s_c.at[w], r_c.at[w], dp=0)
        else:
            for w, g in enumerate(gathered):
                for way, to in enumerate((after, ahead)):
                    send(g.at[z], g.at[z], s_w.at[w], r_w.at[w, way, 0], expert=to)

    @pl.when(core == 1)
    def _():
        ring(-1)

    far_half = pl.ds(pl.multiple_of(2304 * (1 - yh), 128), 2304)
    sends.append(
        send(patches.at[0, :, far_half], pv.at[yh], s_one.at[0], r_one.at[0], expert=far, tensor=across)
    )

    def regroup():
        for i in range(1, 4):
            xx = lax.rem(x + i, 4)
            for h in range(2):
                rows = pl.ds(pl.multiple_of(2048 * h + 512 * xx, 512), 512)
                for k, source in enumerate((gate, up)):
                    send(
                        source.at[0, rows, :],
                        wgu.at[x, pl.ds(512 * h, 512), pl.ds(128 * k, 128)],
                        s_gu, r_gu, tensor=yl * 4 + xx,
                    )
        drains.append((wgu.at[pl.ds(0, 3)], s_gu))
        cols = pl.ds(pl.multiple_of((1 - yh) * 2048 + x * 512 + (1 - yl) * 256, 128), 256)
        sends.append(
            send(text.at[0, :, cols], tx.at[yh], s_one.at[1], r_one.at[1], expert=far, tensor=across)
        )

    def iota(shape, dim):
        return lax.broadcasted_iota(I32, shape, dim)

    def route():
        line = iota((32, 128), 0)
        dist = jnp.zeros((32, 128), I32)
        for p, d in enumerate(DISTANCES):
            dist = jnp.where((line >> 1) == p, d, dist)
        expert = (line & 1) * 16 + ((z + dist) & 15)
        member = jnp.zeros((32, 128), F32)
        share = jnp.zeros((32, 128), F32)
        for k in range(8):
            named = ids[k : k + 1, :] == expert
            member = jnp.where(named, 1.0, member)
            share = share + jnp.where(named, shares[k : k + 1, :], 0.0)
        before = (iota((128, 128), 0) < iota((128, 128), 1)).astype(F32).astype(BF)
        rank = nn(member.astype(BF), before)
        rt[yh] = jnp.where(member > 0.5, rank, -1.0).astype(BF)
        wt[...] = share
        sends.append(send(rt.at[yh], rt.at[yh], s_one.at[2], r_one.at[2], expert=far, tensor=across))

    def images():
        unit_row = units[...].astype(F32)
        first = (iota((32, 32), 0) < iota((32, 32), 1)).astype(F32).astype(BF)
        starts = nn(jnp.broadcast_to(unit_row, (8, 32)).astype(BF), first)[:1]
        slot = iota((128, 32), 0)
        owner = ((slot >> 1) & 1) * 16 + ((z + (slot >> 3)) & 15)
        match = (owners[...] == owner) & (((slot >> 2) & 1) == yh)

        def pick_out(row):
            return jnp.sum(jnp.where(match, row, 0.0), axis=1, keepdims=True)

        start, count = pick_out(starts), pick_out(unit_row)
        offset = pick_out(offsets[...].astype(F32))
        column = iota((128, 1), 0)
        turn = (column & 1).astype(F32)
        valid = turn < count
        base = (yh * 64).astype(F32)
        source = jnp.where(valid, base + start + turn, -1.0)
        position = jnp.where(valid, ((column >> 1) & 1).astype(F32) * 128.0 + offset + turn, -1.0)
        sel_own[...] = (iota((128, 128), 1).astype(F32) == source).astype(F32).astype(BF)
        info_own[...] = jnp.broadcast_to(position, (128, 128)).reshape(16, 8, 128)
        sends.append(send(sel_own, sel_far, s_one.at[3], r_one.at[3], expert=far, tensor=across))
        sends.append(send(info_own, info_far, s_one.at[5], r_one.at[5], expert=far, tensor=across))

    def norm_patches(own, p):
        g = yh if own else 1 - yh
        if p == 0:
            if own:
                local[0].wait()
            else:
                wait(pv.at[g], r_one.at[0])
        part = pl.ds(1152 * p, 1152)
        v = pv[g, :, part].astype(F32)
        center = v - jnp.mean(v, axis=1, keepdims=True)
        variance = jnp.mean(center * center, axis=1, keepdims=True)
        scaled = center * lax.rsqrt(variance + 1e-06) * pgain[...] + pbias[...]
        xn[g, :, part] = scaled.astype(BF)

    def selections():
        wait(rt.at[1 - yh], r_one.at[2])
        for oy in range(2):
            ranks = rt[oy].astype(F32).reshape(32, 1, 128)
            slots = iota((32, 16, 128), 1).astype(F32)
            pick[oy] = (ranks == slots).astype(F32).reshape(512, 128).astype(BF)

    jobs = {
        0: [regroup, route],
        1: [images],
        2: [lambda: norm_patches(True, 0)],
        3: [lambda: norm_patches(True, 1)],
        4: [selections],
        5: [lambda: norm_patches(False, 0)],
        6: [lambda: norm_patches(False, 1)],
    }
    for s in range(8):

        @pl.when(core == 1)
        def _():
            ring(s)

        for job in jobs.get(s, ()):
            job()

    @pl.when(core == 0)
    def _():
        wait(g1.at[pl.ds(0, 15)], r_c.at[0])

    w1x[...] = jnp.zeros((16, 144, 128), BF)
    for r in range(9):
        low = 144 if r < 8 else 160
        w1x[:, 16 * r : 16 * r + 16, :32] = g1[:, low : low + 16, 32 * (r % 8) : 32 * (r % 8) + 32]
    rows = xn[...].reshape(128, 2304)
    main = nn(rows, g1[:, :144, :].reshape(2304, 256))
    tail = nn(rows, w1x[...].reshape(2304, 128))
    p1s[:128] = main.astype(BF)
    for r in range(8):
        p1s[128:144, 32 * r : 32 * r + 32] = tail[16 * r : 16 * r + 16, :32].astype(BF)
    sends.append(send(p1s, p1r, s_one.at[4], r_one.at[4], expert=far))

    @pl.when(core == 0)
    def _():
        wait(g2.at[pl.ds(0, 15)], r_c.at[1])

    wait(sel_far, r_one.at[3])
    wait(info_far, r_one.at[5])
    chosen = sel_own[...] + sel_far[...]
    info_s[...] = jnp.maximum(info_own[...], info_far[...])

    def gelu(v):
        return (0.5 * v * (1.0 + lax.erf(v * (0.5**0.5)))).astype(BF)

    wait(p1r, r_one.at[4])
    hid[:, :256] = gelu(main + p1r[:128].astype(F32) + b1[:, :256])
    for r in range(8):
        far_tail = p1r[128:144, 32 * r : 32 * r + 32].astype(F32)
        hid[16 * r : 16 * r + 16, 256:] = gelu(tail[16 * r : 16 * r + 16, :32] + far_tail + b1[:, 256:])

    def second(tt):
        k = 2 * lax.rem(tt, 4) + tt // 4
        units_here = hid[...]
        return jnp.concatenate([nn(units_here, g2[2 * k]), nn(units_here, g2[2 * k + 1])], axis=1)

    for i in range(1, 8):
        tt = lax.rem(t + i, 8)
        p2s[i - 1] = second(tt).astype(BF)
        send(p2s.at[i - 1], p2r.at[i - 1], s_p2, r_p2, tensor=tt)
    drains.append((p2r.at[pl.ds(0, 7)], s_p2))
    total = second(t) + b2[:, pl.ds(pl.multiple_of(col, 128), 256)]
    for d in range(1, 16):
        send(info_s.at[d], info_r.at[d], s_info, r_info, expert=yh * 16 + lax.rem(z + d, 16))
    info_r[0] = info_s[0]
    drains.append((info_r.at[pl.ds(0, 15)], s_info))
    wait(p2r.at[pl.ds(0, 7)], r_p2)
    for i in range(7):
        total = total + p2r[i].astype(F32)
    emb = total.astype(BF)

    rows = nn(chosen, emb).reshape(16, 8, 256)
    img_s[...] = jnp.concatenate([rows[:, :, :128], rows[:, :, 128:]], axis=1).astype(BF)
    img_r[0] = img_s[0]
    for d in range(1, 16):
        send(img_s.at[d], img_r.at[d], s_img, r_img, expert=yh * 16 + lax.rem(z + d, 16))

    drains.append((img_r.at[pl.ds(0, 15)], s_img))
    local[1].wait()
    wait(tx.at[1 - yh], r_one.at[1])
    wait(info_r.at[pl.ds(0, 15)], r_info)
    position = info_r[...]
    blank = jnp.zeros((16, 8, 128), F32)
    placed = []
    for oy in range(2):
        hit = (position == (iota((16, 8, 128), 2) + oy * 128).astype(F32)).astype(F32)
        low = jnp.concatenate([hit, blank], axis=1).reshape(256, 128).astype(BF)
        high = jnp.concatenate([blank, hit], axis=1).reshape(256, 128).astype(BF)
        covered = tn(low, jnp.ones((256, 128), BF)) > 0.5
        placed.append((low, high, covered))
    wait(img_r.at[pl.ds(0, 15)], r_img)
    arrived = img_r[...].reshape(256, 128)
    for oy in range(2):
        low, high, covered = placed[oy]
        for half, hits in enumerate((low, high)):
            part = pl.ds(128 * half, 128)
            base = tx[oy, :, part].astype(F32)
            st[oy, :, part] = jnp.where(covered, tn(hits, arrived), base).astype(BF)

    for oy in range(2):
        xs[:, :, 16 * oy : 16 * oy + 16, :] = nn(pick[oy], st[oy]).astype(BF).reshape(16, 2, 16, 256)
    for p in range(16):
        if p == HERE:
            continue
        send(xs.at[p], xr.at[p], s_disp, r_disp.at[p], expert=yh * 16 + lax.rem(z + DISTANCES[p], 16))

    drains.append((xr.at[pl.ds(0, 15)], s_disp))

    def forward(c):
        for p in range(PER * c, PER * c + PER):
            if p != HERE:
                wait(xr.at[p], r_disp.at[p])
            block = xs.at[p] if p == HERE else xr.at[p]
            xk[p, y] = block[yh]
            dst = xk.at[p, y]
            send(block.at[yh], dst, s_ag, r_ag.at[c], tensor=across)
            send(block.at[1 - yh], dst, s_ag, r_ag.at[c], expert=far)
            send(block.at[1 - yh], dst, s_ag, r_ag.at[c], expert=far, tensor=across)

    def project(c):
        wait(xk.at[pl.ds(PER * c, 3)], r_ag.at[c])
        if c == 0:
            for copy in local[3:]:
                copy.wait()
            wait(wgu.at[pl.ds(0, 3)], r_gu)
        squares = jnp.zeros((8, ROWS), F32)
        ones = jnp.ones((8, 256), BF)
        for yy in range(4):
            v = xk[PER * c : PER * c + PER, yy].reshape(ROWS, 256).astype(F32)
            start = 2048 * (yy // 2) + 256 * (yy % 2) + 512 * x
            gain = tgain[:, pl.ds(pl.multiple_of(start, 128), 256)]
            gx[:, 256 * yy : 256 * yy + 256] = (v * gain).astype(BF)
            square = v * v
            high = square.astype(BF)
            low = (square - high.astype(F32)).astype(BF)
            squares = squares + nt(ones, high) + nt(ones, low)
        ss_s[c] = squares
        for i in range(1, 4):
            xx = lax.rem(x + i, 4)
            send(ss_s.at[c], ss_r.at[c, i - 1], s_ss, r_ss.at[c], tensor=yl * 4 + xx)
            ps[c, i] = nn(gx[...], wgu[xx]).astype(BF)
            send(ps.at[c, i], pr.at[c, i - 1], s_rs, r_rs.at[c], tensor=yl * 4 + xx)
        ps[c, 0] = nn(gx[...], wgu[x]).astype(BF)

    def activate(c):
        wait(ss_r.at[c], r_ss.at[c])
        wait(pr.at[c], r_rs.at[c])
        squares = ss_s[c, 0:1] + ss_r[c, 0, 0:1] + ss_r[c, 1, 0:1] + ss_r[c, 2, 0:1]
        inverse = lax.rsqrt(squares * (1.0 / 4096.0) + 1e-06)
        eye = iota((ROWS, ROWS), 0) == iota((ROWS, ROWS), 1)
        inverse = jnp.sum(jnp.where(eye, inverse, 0.0), axis=1, keepdims=True)
        sums = ps[c, 0].astype(F32) + pr[c, 0].astype(F32) + pr[c, 1].astype(F32) + pr[c, 2].astype(F32)
        sums = sums * inverse
        gated, upped = sums[:, :128], sums[:, 128:]
        activation = (gated / (1.0 + jnp.exp(-gated)) * upped).astype(BF)
        act_s[c] = activation
        mine = pl.ds(pl.multiple_of(t * 128, 128), 128)
        act_r[c, :, mine] = activation
        for i in range(1, 8):
            send(act_s.at[c], act_r.at[c, :, mine], s_act, r_act.at[c], tensor=lax.rem(t + i, 8))

    def produce(c):
        if c == 0:
            local[2].wait()
        wait(act_r.at[c, :, pl.ds(0, 896)], r_act.at[c])
        ob[PER * c : PER * c + PER] = nn(act_r[c], dw[...]).astype(BF).reshape(PER, 2, 16, 512)
        for p in range(PER * c, PER * c + PER):
            zz = lax.rem(z - DISTANCES[p] + 16, 16)
            dst = rb.at[2 * p + yh]
            if p == HERE:
                rb[2 * p + yh] = ob[p, yh]
                send(ob.at[p, 1 - yh], dst, s_ret, r_ret, expert=far)
            else:
                for oy in range(2):
                    send(ob.at[p, oy], dst, s_ret, r_ret, expert=oy * 16 + zz)

    for turn in range(CHUNKS + 4):
        if turn < CHUNKS:
            forward(turn)
        if 0 <= turn - 1 < CHUNKS:
            project(turn - 1)
        if 0 <= turn - 2 < CHUNKS:
            activate(turn - 2)
        if 0 <= turn - 3 < CHUNKS:
            produce(turn - 3)

    drains.append((xk.at[pl.ds(0, 12)], s_ag))
    drains.append((pr, s_rs))
    drains.append((ss_r, s_ss))
    drains.append((act_r.at[:, :, pl.ds(0, 896)], s_act))
    drains.append((rb.at[pl.ds(0, 31)], s_ret))
    weight = pick[yh].astype(F32).reshape(32, 16, 128) * wt[...].reshape(32, 1, 128)
    weight = weight.reshape(512, 128)
    high = weight.astype(BF)
    low = (weight - high.astype(F32)).astype(BF)
    wait(rb.at[pl.ds(0, 31)], r_ret)
    back = rb[...].reshape(512, 512)
    out[0] = (tn(high, back) + tn(low, back)).astype(BF)

    finish()


def body(
    patches, patch_gain, patch_bias, first_weight, first_bias, second_weight, second_bias,
    image_units, image_owner, image_offset, text_states, token_gain, expert_ids,
    route_weights, gate_weight, up_weight, down_weight,
):
    vmem = pl.BlockSpec(memory_space=pltpu.VMEM)
    hbm = pl.BlockSpec(memory_space=pltpu.HBM)
    dma = pltpu.SemaphoreType.DMA
    scratch = [
        pltpu.VMEM((16, 176, 256), BF),
        pltpu.VMEM((16, 288, 128), BF),
        pltpu.VMEM((16, 144, 128), BF),
        pltpu.VMEM((2, 64, 2304), BF),
        pltpu.VMEM((2, 64, 2304), BF),
        pltpu.VMEM((128, 288), BF),
        pltpu.VMEM((144, 256), BF),
        pltpu.VMEM((144, 256), BF),
        pltpu.VMEM((7, 128, 256), BF),
        pltpu.VMEM((7, 128, 256), BF),
        pltpu.VMEM((128, 128), BF),
        pltpu.VMEM((128, 128), BF),
        pltpu.VMEM((16, 8, 128), F32),
        pltpu.VMEM((16, 8, 128), F32),
        pltpu.VMEM((16, 8, 128), F32),
        pltpu.VMEM((16, 8, 128), F32),
        pltpu.VMEM((16, 16, 128), BF),
        pltpu.VMEM((16, 16, 128), BF),
        pltpu.VMEM((2, 128, 256), BF),
        pltpu.VMEM((2, 32, 128), BF),
        pltpu.VMEM((32, 128), F32),
        pltpu.VMEM((2, 512, 128), BF),
        pltpu.VMEM((2, 128, 256), BF),
        pltpu.VMEM((16, 2, 32, 256), BF),
        pltpu.VMEM((16, 2, 32, 256), BF),
        pltpu.VMEM((16, 4, 32, 256), BF),
        pltpu.VMEM((4, 1024, 256), BF),
        pltpu.VMEM((1024, 512), BF),
        pltpu.VMEM((ROWS, 1024), BF),
        pltpu.VMEM((CHUNKS, 4, ROWS, 256), BF),
        pltpu.VMEM((CHUNKS, 3, ROWS, 256), BF),
        pltpu.VMEM((CHUNKS, 8, ROWS), F32),
        pltpu.VMEM((CHUNKS, 3, 8, ROWS), F32),
        pltpu.VMEM((CHUNKS, ROWS, 128), BF),
        pltpu.VMEM((CHUNKS, ROWS, 1024), BF),
        pltpu.VMEM((16, 2, 16, 512), BF),
        pltpu.VMEM((32, 16, 512), BF),
        dma((2,)), dma((2, 2, 8)), dma((2,)), dma((2,)),
        dma((7,)), dma, dma, dma((6,)), dma((6,)),
        dma, dma, dma, dma, dma, dma,
        dma, dma((16,)), dma, dma((CHUNKS,)),
        dma, dma((CHUNKS,)), dma, dma((CHUNKS,)), dma, dma((CHUNKS,)),
        dma, dma,
    ]
    call = pl.pallas_call(
        kernel,
        out_shape=jax.ShapeDtypeStruct((1, 128, 512), BF),
        in_specs=[
            hbm, vmem, vmem, vmem, vmem, vmem, vmem, vmem, vmem, vmem, hbm, vmem,
            vmem, vmem, hbm, hbm, hbm,
        ],
        out_specs=vmem,
        scratch_shapes=scratch,
        compiler_params=pltpu.CompilerParams(
            collective_id=0, has_side_effects=True, vmem_limit_bytes=60 * 1024 * 1024
        ),
    )
    return call(
        patches, patch_gain[None], patch_bias[None], first_weight, first_bias[None],
        second_weight.T, second_bias[None], image_units, image_owner, image_offset,
        text_states, token_gain[None], expert_ids[0].T, route_weights[0].T,
        gate_weight, up_weight, down_weight,
    )


def solution(mesh):
    in_specs = (
        P(("dp", "expert"), None, None),
        P(),
        P(),
        P("expert", "tensor"),
        P("tensor"),
        P("expert", "tensor"),
        P(),
        P(("dp", "expert"), None),
        P(("dp", "expert"), None),
        P(("dp", "expert"), None),
        P(("dp", "expert"), None, None),
        P(),
        P(("dp", "expert"), None, None),
        P(("dp", "expert"), None, None),
        P("expert", None, "tensor"),
        P("expert", None, "tensor"),
        P("expert", None, "tensor"),
    )
    out_specs = P(("dp", "expert"), None, "tensor")
    return jax.shard_map(body, mesh=mesh, in_specs=in_specs, out_specs=out_specs, check_vma=False)
```

```python
import jax
import jax.numpy as jnp
from jax import lax
from jax.experimental import pallas as pl
from jax.experimental.pallas import tpu as pltpu
from jax.sharding import PartitionSpec as P

BF = jnp.bfloat16
F32 = jnp.float32
I32 = jnp.int32
MESH = pl.DeviceIdType.MESH

PLANES = 16
CHUNKS = 4
PER = PLANES // CHUNKS
ROWS = PER * 32


DISTANCES = (0, 8, 1, 15, 7, 9, 2, 14, 6, 10, 3, 13, 5, 11, 4, 12)
HERE = DISTANCES.index(0)


def nn(a, b):
    return jnp.dot(a, b, preferred_element_type=F32)


def nt(a, b):
    return lax.dot_general(a, b, (((1,), (1,)), ((), ())), preferred_element_type=F32)


def tn(a, b):
    return lax.dot_general(a, b, (((0,), (0,)), ((), ())), preferred_element_type=F32)


def wait(ref, sem):
    pltpu.make_async_copy(ref, ref, sem).wait()


def kernel(
    patches, pgain, pbias, w1, b1, w2, b2, units, owners, offsets, text, tgain,
    ids, shares, gate, up, down,
    out,
    g1, g2, w1x, pv, xz, hid, p1s, p1r, p2s, p2r, swap_own, swap_far, info_s, info_r,
    img_s, img_r, tx, wt, pick, st, xs, xr, xk, wgu, dw, gx, ps, pr, ss, act_s, act_r, ob, rb,
    s_w, r_w, s_c, r_c, l_sem, s_gu, r_gu, s_one, r_one, s_info, r_info, s_p2, r_p2,
    s_img, r_img, s_disp, r_disp, s_ag, r_ag, s_rs, r_rs, s_act, r_act,
    s_ret, r_ret,
):
    e = lax.axis_index("expert")
    t = lax.axis_index("tensor")
    core = lax.axis_index("dp")
    yh, z = e // 16, e % 16
    yl, x = t // 4, t % 4
    y = 2 * yh + yl
    far = (1 - yh) * 16 + z
    col = yh * 2048 + x * 512 + yl * 256

    def send(src, dst, ssem, rsem, **dev):
        copy = pltpu.make_async_remote_copy(
            src_ref=src, dst_ref=dst, send_sem=ssem, recv_sem=rsem,
            device_id=dev, device_id_type=MESH,
        )
        copy.start()
        return copy

    local = [
        (patches.at[0, :, pl.ds(pl.multiple_of(2304 * yh, 128), 2304)], pv.at[yh]),
        (text.at[0, :, pl.ds(pl.multiple_of(col, 128), 256)], tx.at[yh]),
        (down.at[0], dw),
    ]
    for k, source in enumerate((gate, up)):
        local.append((source.at[:, x], wgu.at[x, :, :, pl.ds(128 * k, 128)]))
    local = [pltpu.make_async_copy(a, b, l_sem.at[i]) for i, (a, b) in enumerate(local)]
    for copy in local:
        copy.start()

    barrier = pltpu.get_barrier_semaphore()
    after = yh * 16 + lax.rem(z + 1, 16)
    ahead = yh * 16 + lax.rem(z + 15, 16)
    across = lax.rem(t + 4, 8)

    def greet(**dev):
        pl.semaphore_signal(barrier, inc=1, device_id=dev, device_id_type=MESH)

    greet(expert=after)
    greet(expert=ahead)
    greet(dp=1 - core)
    for i in range(1, 8):
        greet(tensor=lax.rem(t + i, 8))
    greet(expert=far)
    greet(expert=far, tensor=across)

    g1[0, :144, :] = w1[:, :256]
    for r in range(9):
        low = 144 if r < 8 else 160
        g1[0, low : low + 16, 32 * (r % 8) : 32 * (r % 8) + 32] = w1[16 * r : 16 * r + 16, 256:288]
    g2[0] = w2[...]

    pl.semaphore_wait(barrier, 12)

    sends, drains = [], []

    def finish():
        for copy in sends:
            copy.wait_send()
        for ref, sem in drains:
            wait(ref, sem)

        @pl.when(core == 1)
        def _():
            for w, g in enumerate(gathered):
                wait(g.at[pl.ds(1, 15)], s_w.at[w])
                wait(g.at[pl.ds(1, 15)], s_c.at[w])

    gathered = (g1, g2)

    def hand_on(first, count):
        for w, g in enumerate(gathered):
            blocks = g.at[pl.ds(first, count)]
            send(blocks, blocks, s_c.at[w], r_c.at[w], dp=0)

    def ring(step):
        for w, g in enumerate(gathered):
            for way, to in enumerate((after, ahead)):
                if step < 8 - way:
                    here, there = (step, step + 1) if way == 0 else ((16 - step) % 16, 15 - step)
                    if step > 0:
                        wait(g.at[here], r_w.at[w, way, step - 1])
                    send(g.at[here], g.at[there], s_w.at[w], r_w.at[w, way, step], expert=to)
                elif step == 8 - way:
                    here = step if way == 0 else 16 - step
                    wait(g.at[here], r_w.at[w, way, step - 1])
        if step == 3:
            hand_on(1, 3)
            hand_on(13, 3)
        if step == 6:
            hand_on(4, 3)
            hand_on(10, 3)
        if step == 8:
            hand_on(7, 3)

    @pl.when(core == 1)
    def _():
        ring(0)

    far_half = pl.ds(pl.multiple_of(2304 * (1 - yh), 128), 2304)
    sends.append(
        send(patches.at[0, :, far_half], pv.at[yh], s_one.at[0], r_one.at[0], expert=far, tensor=across)
    )

    def regroup():
        for i in range(1, 4):
            xx = lax.rem(x + i, 4)
            for k, source in enumerate((gate, up)):
                dst = wgu.at[x, :, :, pl.ds(128 * k, 128)]
                send(source.at[:, xx], dst, s_gu, r_gu, tensor=yl * 4 + xx)
        drains.append((wgu.at[pl.ds(0, 3)], s_gu))
        cols = pl.ds(pl.multiple_of((1 - yh) * 2048 + x * 512 + (1 - yl) * 256, 128), 256)
        sends.append(
            send(text.at[0, :, cols], tx.at[yh], s_one.at[1], r_one.at[1], expert=far, tensor=across)
        )

    def iota(shape, dim):
        return lax.broadcasted_iota(I32, shape, dim)

    def route():
        line = iota((32, 128), 0)
        dist = jnp.zeros((32, 128), I32)
        for p, d in enumerate(DISTANCES):
            dist = jnp.where((line >> 1) == p, d, dist)
        expert = (line & 1) * 16 + ((z + dist) & 15)
        member = jnp.zeros((32, 128), F32)
        share = jnp.zeros((32, 128), F32)
        for k in range(8):
            named = ids[k : k + 1, :] == expert
            member = jnp.where(named, 1.0, member)
            share = share + jnp.where(named, shares[k : k + 1, :], 0.0)
        before = (iota((128, 128), 0) < iota((128, 128), 1)).astype(F32).astype(BF)
        rank = nn(member.astype(BF), before)
        swap_own[256:288] = jnp.where(member > 0.5, rank, -1.0).astype(BF)
        wt[...] = share

    def images():
        unit_row = units[...].astype(F32)
        first = (iota((32, 32), 0) < iota((32, 32), 1)).astype(F32).astype(BF)
        starts = nn(jnp.broadcast_to(unit_row, (8, 32)).astype(BF), first)[:1]
        slot = iota((128, 32), 0)
        owner = ((slot >> 1) & 1) * 16 + ((z + (slot >> 3)) & 15)
        match = (owners[...] == owner) & (((slot >> 2) & 1) == yh)

        def pick_out(row):
            return jnp.sum(jnp.where(match, row, 0.0), axis=1, keepdims=True)

        start, count = pick_out(starts), pick_out(unit_row)
        offset = pick_out(offsets[...].astype(F32))
        column = iota((128, 1), 0)
        turn = (column & 1).astype(F32)
        valid = turn < count
        base = (yh * 64).astype(F32)
        source = jnp.where(valid, base + start + turn, -1.0)
        position = jnp.where(valid, ((column >> 1) & 1).astype(F32) * 128.0 + offset + turn, -1.0)
        swap_own[:128] = (iota((128, 128), 1).astype(F32) == source).astype(F32).astype(BF)
        swap_own[128:256] = jnp.broadcast_to(position, (128, 128)).astype(BF)
        sends.append(send(swap_own, swap_far, s_one.at[2], r_one.at[2], expert=far, tensor=across))

    def norm_patches(own, p):
        g = yh if own else 1 - yh
        if p == 0:
            if own:
                local[0].wait()
            else:
                wait(pv.at[g], r_one.at[0])
        part = pl.ds(1152 * p, 1152)
        v = pv[g, :, part].astype(F32)
        center = v - jnp.mean(v, axis=1, keepdims=True)
        variance = jnp.mean(center * center, axis=1, keepdims=True)
        scaled = center * lax.rsqrt(variance + 1e-06) * pgain[...] + pbias[...]
        for o in range(8):
            xz[8 * p + o, g] = scaled[:, 144 * o : 144 * o + 144].astype(BF)

    def selections():
        wait(swap_far, r_one.at[2])
        for oy, swap in ((yh, swap_own), (1 - yh, swap_far)):
            ranks = swap[256:288].astype(F32).reshape(32, 1, 128)
            slots = iota((32, 16, 128), 1).astype(F32)
            pick[oy] = (ranks == slots).astype(F32).reshape(512, 128).astype(BF)
        positions = jnp.maximum(swap_own[128:256].astype(F32), swap_far[128:256].astype(F32))
        info_s[...] = positions.reshape(16, 8, 128)

    jobs = {
        0: [regroup, route],
        1: [images],
        2: [lambda: norm_patches(True, 0)],
        3: [lambda: norm_patches(True, 1)],
        4: [selections],
        5: [lambda: norm_patches(False, 0)],
        6: [lambda: norm_patches(False, 1)],
    }
    for s in range(8):

        @pl.when(core == 1)
        def _():
            ring(s + 1)

        for job in jobs.get(s, ()):
            job()

    @pl.when(core == 0)
    def _():
        wait(g1.at[pl.ds(1, 15)], r_c.at[0])

    w1x[...] = jnp.zeros((16, 144, 128), BF)
    for r in range(9):
        low = 144 if r < 8 else 160
        w1x[:, 16 * r : 16 * r + 16, :32] = g1[:, low : low + 16, 32 * (r % 8) : 32 * (r % 8) + 32]
    main, tail = jnp.zeros((128, 256), F32), jnp.zeros((128, 128), F32)
    for r in range(16):
        rows = xz[lax.rem(z - r + 16, 16)].reshape(128, 144)
        main = main + nn(rows, g1[r, :144, :])
        tail = tail + nn(rows, w1x[r])
    p1s[:128] = main.astype(BF)
    for r in range(8):
        p1s[128:144, 32 * r : 32 * r + 32] = tail[16 * r : 16 * r + 16, :32].astype(BF)
    sends.append(send(p1s, p1r, s_one.at[3], r_one.at[3], expert=far))
    for d in range(1, 16):
        send(info_s.at[d], info_r.at[d], s_info, r_info, expert=yh * 16 + lax.rem(z + d, 16))
    info_r[0] = info_s[0]
    drains.append((info_r.at[pl.ds(0, 15)], s_info))

    @pl.when(core == 0)
    def _():
        wait(g2.at[pl.ds(1, 15)], r_c.at[1])

    chosen = swap_own[:128] + swap_far[:128]

    def gelu(v):
        return (0.5 * v * (1.0 + lax.erf(v * (0.5**0.5)))).astype(BF)

    wait(p1r, r_one.at[3])
    hid[:, :256] = gelu(main + p1r[:128].astype(F32) + b1[:, :256])
    for r in range(8):
        far_tail = p1r[128:144, 32 * r : 32 * r + 32].astype(F32)
        hid[16 * r : 16 * r + 16, 256:] = gelu(tail[16 * r : 16 * r + 16, :32] + far_tail + b1[:, 256:])

    def second(tt):
        k = 2 * lax.rem(tt, 4) + tt // 4
        units_here = hid[...]
        return jnp.concatenate([nn(units_here, g2[lax.rem(z - 2 * k + 16, 16)]), nn(units_here, g2[lax.rem(z - 2 * k + 15, 16)])], axis=1)

    for i in range(1, 8):
        tt = lax.rem(t + i, 8)
        p2s[i - 1] = second(tt).astype(BF)
        send(p2s.at[i - 1], p2r.at[i - 1], s_p2, r_p2, tensor=tt)
    drains.append((p2r.at[pl.ds(0, 7)], s_p2))
    total = second(t) + b2[:, pl.ds(pl.multiple_of(col, 128), 256)]
    wait(p2r.at[pl.ds(0, 7)], r_p2)
    for i in range(7):
        total = total + p2r[i].astype(F32)
    emb = total.astype(BF)

    rows = nn(chosen, emb).reshape(16, 8, 256)
    img_s[...] = jnp.concatenate([rows[:, :, :128], rows[:, :, 128:]], axis=1).astype(BF)
    img_r[0] = img_s[0]
    for d in range(1, 16):
        send(img_s.at[d], img_r.at[d], s_img, r_img, expert=yh * 16 + lax.rem(z + d, 16))

    drains.append((img_r.at[pl.ds(0, 15)], s_img))
    local[1].wait()
    wait(tx.at[1 - yh], r_one.at[1])
    wait(info_r.at[pl.ds(0, 15)], r_info)
    position = info_r[...]
    blank = jnp.zeros((16, 8, 128), F32)
    placed = []
    for oy in range(2):
        hit = (position == (iota((16, 8, 128), 2) + oy * 128).astype(F32)).astype(F32)
        low = jnp.concatenate([hit, blank], axis=1).reshape(256, 128).astype(BF)
        high = jnp.concatenate([blank, hit], axis=1).reshape(256, 128).astype(BF)
        covered = tn(low, jnp.ones((256, 128), BF)) > 0.5
        placed.append((low, high, covered))
    wait(img_r.at[pl.ds(0, 15)], r_img)
    arrived = img_r[...].reshape(256, 128)
    for oy in range(2):
        low, high, covered = placed[oy]
        for half, hits in enumerate((low, high)):
            part = pl.ds(128 * half, 128)
            base = tx[oy, :, part].astype(F32)
            st[oy, :, part] = jnp.where(covered, tn(hits, arrived), base).astype(BF)

    for oy in range(2):
        xs[:, :, 16 * oy : 16 * oy + 16, :] = nn(pick[oy], st[oy]).astype(BF).reshape(16, 2, 16, 256)
    for p in range(16):
        if p == HERE:
            continue
        send(xs.at[p], xr.at[p], s_disp, r_disp.at[p], expert=yh * 16 + lax.rem(z + DISTANCES[p], 16))

    drains.append((xr.at[pl.ds(0, 15)], s_disp))

    def forward(c):
        part = pl.ds(PER * c, PER)
        for p in range(PER * c, PER * c + PER):
            if p == HERE:
                xr[p] = xs[p]
            else:
                wait(xr.at[p], r_disp.at[p])
        dst = xk.at[part, y]
        send(xr.at[part, 1 - yh], dst, s_ag, r_ag.at[c], expert=far)
        send(xr.at[part, 1 - yh], dst, s_ag, r_ag.at[c], expert=far, tensor=across)
        send(xr.at[part, yh], dst, s_ag, r_ag.at[c], tensor=across)
        xk[part, y] = xr[part, yh]

    def project(c):
        wait(xk.at[pl.ds(PER * c, PER), pl.ds(0, 3)], r_ag.at[c])
        if c == 0:
            for copy in local[3:]:
                copy.wait()
            wait(wgu.at[pl.ds(0, 3)], r_gu)
        squares = jnp.zeros((8, ROWS), F32)
        ones = jnp.ones((8, 256), BF)
        for yy in range(4):
            v = xk[PER * c : PER * c + PER, yy].reshape(ROWS, 256).astype(F32)
            start = 2048 * (yy // 2) + 256 * (yy % 2) + 512 * x
            gain = tgain[:, pl.ds(pl.multiple_of(start, 128), 256)]
            gx[:, 256 * yy : 256 * yy + 256] = (v * gain).astype(BF)
            square = v * v
            high = square.astype(BF)
            low = (square - high.astype(F32)).astype(BF)
            squares = squares + nt(ones, high) + nt(ones, low)
        ss[c] = squares
        high = squares.astype(BF).astype(F32)
        squares = jnp.concatenate([high, squares - high], axis=0).astype(BF)
        for i in range(1, 4):
            xx = lax.rem(x + i, 4)
            ps[c, i, :ROWS] = nn(gx[...], wgu[xx].reshape(1024, 256)).astype(BF)
            ps[c, i, ROWS:, :ROWS] = squares
            send(ps.at[c, i], pr.at[c, i - 1], s_rs, r_rs.at[c], tensor=yl * 4 + xx)
        ps[c, 0, :ROWS] = nn(gx[...], wgu[x].reshape(1024, 256)).astype(BF)

    def activate(c):
        wait(pr.at[c], r_rs.at[c])
        squares = ss[c, 0:1]
        sums = ps[c, 0, :ROWS].astype(F32)
        for i in range(3):
            both = pr[c, i, ROWS:, :ROWS].astype(F32)
            squares = squares + both[0:1] + both[8:9]
            sums = sums + pr[c, i, :ROWS].astype(F32)
        inverse = lax.rsqrt(squares * (1.0 / 4096.0) + 1e-06)
        eye = iota((ROWS, ROWS), 0) == iota((ROWS, ROWS), 1)
        inverse = jnp.sum(jnp.where(eye, inverse, 0.0), axis=1, keepdims=True)
        sums = sums * inverse
        gated, upped = sums[:, :128], sums[:, 128:]
        activation = (gated / (1.0 + jnp.exp(-gated)) * upped).astype(BF)
        act_s[c] = activation
        mine = pl.ds(pl.multiple_of(t * 128, 128), 128)
        act_r[c, :, mine] = activation
        for i in range(1, 8):
            send(act_s.at[c], act_r.at[c, :, mine], s_act, r_act.at[c], tensor=lax.rem(t + i, 8))

    def produce(c):
        if c == 0:
            local[2].wait()
        wait(act_r.at[c, :, pl.ds(0, 896)], r_act.at[c])
        ob[PER * c : PER * c + PER] = nn(act_r[c], dw[...]).astype(BF).reshape(PER, 2, 16, 512)
        for p in range(PER * c, PER * c + PER):
            zz = lax.rem(z - DISTANCES[p] + 16, 16)
            dst = rb.at[2 * p + yh]
            if p == HERE:
                rb[2 * p + yh] = ob[p, yh]
                send(ob.at[p, 1 - yh], dst, s_ret, r_ret, expert=far)
            else:
                for oy in range(2):
                    send(ob.at[p, oy], dst, s_ret, r_ret, expert=oy * 16 + zz)

    for turn in range(CHUNKS + 4):
        if turn < CHUNKS:
            forward(turn)
        if 0 <= turn - 1 < CHUNKS:
            project(turn - 1)
        if 0 <= turn - 2 < CHUNKS:
            activate(turn - 2)
        if 0 <= turn - 3 < CHUNKS:
            produce(turn - 3)

    drains.append((xk.at[:, pl.ds(0, 3)], s_ag))
    drains.append((pr, s_rs))
    drains.append((act_r.at[:, :, pl.ds(0, 896)], s_act))
    drains.append((rb.at[pl.ds(0, 31)], s_ret))
    weight = pick[yh].astype(F32).reshape(32, 16, 128) * wt[...].reshape(32, 1, 128)
    weight = weight.reshape(512, 128)
    high = weight.astype(BF)
    low = (weight - high.astype(F32)).astype(BF)
    wait(rb.at[pl.ds(0, 31)], r_ret)
    back = rb[...].reshape(512, 512)
    out[0] = (tn(high, back) + tn(low, back)).astype(BF)

    finish()


def body(
    patches, patch_gain, patch_bias, first_weight, first_bias, second_weight, second_bias,
    image_units, image_owner, image_offset, text_states, token_gain, expert_ids,
    route_weights, gate_weight, up_weight, down_weight,
):
    vmem = pl.BlockSpec(memory_space=pltpu.VMEM)
    hbm = pl.BlockSpec(memory_space=pltpu.HBM)
    dma = pltpu.SemaphoreType.DMA
    scratch = [
        pltpu.VMEM((16, 176, 256), BF),
        pltpu.VMEM((16, 288, 128), BF),
        pltpu.VMEM((16, 144, 128), BF),
        pltpu.VMEM((2, 64, 2304), BF),
        pltpu.VMEM((16, 2, 64, 144), BF),
        pltpu.VMEM((128, 288), BF),
        pltpu.VMEM((144, 256), BF),
        pltpu.VMEM((144, 256), BF),
        pltpu.VMEM((7, 128, 256), BF),
        pltpu.VMEM((7, 128, 256), BF),
        pltpu.VMEM((288, 128), BF),
        pltpu.VMEM((288, 128), BF),
        pltpu.VMEM((16, 8, 128), F32),
        pltpu.VMEM((16, 8, 128), F32),
        pltpu.VMEM((16, 16, 128), BF),
        pltpu.VMEM((16, 16, 128), BF),
        pltpu.VMEM((2, 128, 256), BF),
        pltpu.VMEM((32, 128), F32),
        pltpu.VMEM((2, 512, 128), BF),
        pltpu.VMEM((2, 128, 256), BF),
        pltpu.VMEM((16, 2, 32, 256), BF),
        pltpu.VMEM((16, 2, 32, 256), BF),
        pltpu.VMEM((16, 4, 32, 256), BF),
        pltpu.VMEM((4, 2, 512, 256), BF),
        pltpu.VMEM((1024, 512), BF),
        pltpu.VMEM((ROWS, 1024), BF),
        pltpu.VMEM((CHUNKS, 4, ROWS + 16, 256), BF),
        pltpu.VMEM((CHUNKS, 3, ROWS + 16, 256), BF),
        pltpu.VMEM((CHUNKS, 8, ROWS), F32),
        pltpu.VMEM((CHUNKS, ROWS, 128), BF),
        pltpu.VMEM((CHUNKS, ROWS, 1024), BF),
        pltpu.VMEM((16, 2, 16, 512), BF),
        pltpu.VMEM((32, 16, 512), BF),
        dma((2,)), dma((2, 2, 8)), dma((2,)), dma((2,)),
        dma((5,)), dma, dma, dma((4,)), dma((4,)),
        dma, dma, dma, dma, dma, dma,
        dma, dma((16,)), dma, dma((CHUNKS,)),
        dma, dma((CHUNKS,)), dma, dma((CHUNKS,)),
        dma, dma,
    ]
    call = pl.pallas_call(
        kernel,
        out_shape=jax.ShapeDtypeStruct((1, 128, 512), BF),
        in_specs=[
            hbm, vmem, vmem, vmem, vmem, vmem, vmem, vmem, vmem, vmem, hbm, vmem,
            vmem, vmem, hbm, hbm, hbm,
        ],
        out_specs=vmem,
        scratch_shapes=scratch,
        compiler_params=pltpu.CompilerParams(
            collective_id=0, has_side_effects=True, vmem_limit_bytes=60 * 1024 * 1024
        ),
    )
    return call(
        patches, patch_gain[None], patch_bias[None], first_weight, first_bias[None],
        second_weight.T, second_bias[None], image_units, image_owner, image_offset,
        text_states, token_gain[None], expert_ids[0].T, route_weights[0].T,
        gate_weight.reshape(2, 4, 512, 128), up_weight.reshape(2, 4, 512, 128), down_weight,
    )


def solution(mesh):
    in_specs = (
        P(("dp", "expert"), None, None),
        P(),
        P(),
        P("expert", "tensor"),
        P("tensor"),
        P("expert", "tensor"),
        P(),
        P(("dp", "expert"), None),
        P(("dp", "expert"), None),
        P(("dp", "expert"), None),
        P(("dp", "expert"), None, None),
        P(),
        P(("dp", "expert"), None, None),
        P(("dp", "expert"), None, None),
        P("expert", None, "tensor"),
        P("expert", None, "tensor"),
        P("expert", None, "tensor"),
    )
    out_specs = P(("dp", "expert"), None, "tensor")
    return jax.shard_map(body, mesh=mesh, in_specs=in_specs, out_specs=out_specs, check_vma=False)
```

```python
import jax
import jax.numpy as jnp
from jax import lax
from jax.experimental import pallas as pl
from jax.experimental.pallas import tpu as pltpu
from jax.sharding import PartitionSpec as P

BF = jnp.bfloat16
F32 = jnp.float32
I32 = jnp.int32
MESH = pl.DeviceIdType.MESH

PLANES = 16
CHUNKS = 8
PER = PLANES // CHUNKS
ROWS = PER * 32
PARTS = CHUNKS + 1
FULL = CHUNKS - 1
MOVED = PER * FULL


DISTANCES = (0, 8, 1, 15, 7, 9, 2, 14, 6, 10, 3, 13, 5, 11, 4, 12)
HERE = DISTANCES.index(0)


def nn(a, b):
    return jnp.dot(a, b, preferred_element_type=F32)


def nt(a, b):
    return lax.dot_general(a, b, (((1,), (1,)), ((), ())), preferred_element_type=F32)


def tn(a, b):
    return lax.dot_general(a, b, (((0,), (0,)), ((), ())), preferred_element_type=F32)


def wait(ref, sem):
    pltpu.make_async_copy(ref, ref, sem).wait()


def kernel(
    patches, pgain, pbias, w1, b1, w2, b2, units, owners, offsets, text, tgain,
    ids, shares, gate, up, down,
    out,
    g1, g2, w1x, pv, xz, hid, p1s, p1r, p2s, p2r, swap_own, swap_far, info_s, info_r,
    img_s, img_r, tx, wt, pick, st, xs, xr, xk, wgu, dw, gx, ps, pr, ss, act_s, act_r, ob, rb,
    s_w, r_w, s_c, r_c, l_sem, s_gu, r_gu, s_one, r_one, s_info, r_info, s_p2, r_p2,
    s_img, r_img, s_disp, r_disp, s_ag, r_ag, s_rs, r_rs, s_act, r_act,
    s_ret, r_ret, s_moved,
):
    e = lax.axis_index("expert")
    t = lax.axis_index("tensor")
    core = lax.axis_index("dp")
    yh, z = e // 16, e % 16
    yl, x = t // 4, t % 4
    y = 2 * yh + yl
    far = (1 - yh) * 16 + z
    col = yh * 2048 + x * 512 + yl * 256

    def send(src, dst, ssem, rsem, **dev):
        copy = pltpu.make_async_remote_copy(
            src_ref=src, dst_ref=dst, send_sem=ssem, recv_sem=rsem,
            device_id=dev, device_id_type=MESH,
        )
        copy.start()
        return copy

    local = [
        (patches.at[0, :, pl.ds(pl.multiple_of(2304 * yh, 128), 2304)], pv.at[yh]),
        (text.at[0, :, pl.ds(pl.multiple_of(col, 128), 256)], tx.at[yh]),
        (down.at[0], dw),
    ]
    for k, source in enumerate((gate, up)):
        local.append((source.at[:, x], wgu.at[x, :, :, pl.ds(128 * k, 128)]))
    local = [pltpu.make_async_copy(a, b, l_sem.at[i]) for i, (a, b) in enumerate(local)]
    barrier = pltpu.get_barrier_semaphore()
    after = yh * 16 + lax.rem(z + 1, 16)
    ahead = yh * 16 + lax.rem(z + 15, 16)
    across = lax.rem(t + 4, 8)

    def greet(**dev):
        pl.semaphore_signal(barrier, inc=1, device_id=dev, device_id_type=MESH)

    greet(expert=after)
    greet(expert=ahead)
    greet(dp=1 - core)
    for i in range(1, 8):
        greet(tensor=lax.rem(t + i, 8))
    greet(expert=far)
    greet(expert=far, tensor=across)

    for copy in local:
        copy.start()

    g1[0, :144, :] = w1[:, :256]
    for r in range(9):
        low = 144 if r < 8 else 160
        g1[0, low : low + 16, 32 * (r % 8) : 32 * (r % 8) + 32] = w1[16 * r : 16 * r + 16, 256:288]
    g2[0] = w2[...]

    pl.semaphore_wait(barrier, 12)

    sends, drains = [], []

    def finish():
        for copy in sends:
            copy.wait_send()
        for ref, sem in drains:
            wait(ref, sem)

        for w, g in enumerate(gathered):

            @pl.when(core == 1)
            def _(w=w, g=g):
                wait(g.at[pl.ds(1, 15)], s_w.at[w])
                wait(g.at[pl.ds(1, 15)], s_c.at[w])

    gathered = (g1, g2)
    pieces = (((0, 0, 96), (1, 96, 80)), ((2, 0, 288),))

    def ring(w, step):
        g = gathered[w]

        def hand_on(first, count):
            blocks = g.at[pl.ds(first, count)]
            send(blocks, blocks, s_c.at[w], r_c.at[w], dp=0)

        for k, low, size in pieces[w]:
            rows = pl.ds(low, size)
            for way, to in enumerate((after, ahead)):
                if step < 8 - way:
                    here, there = (step, step + 1) if way == 0 else ((16 - step) % 16, 15 - step)
                    if step > 0:
                        wait(g.at[here, rows], r_w.at[k, way, step - 1])
                    send(g.at[here, rows], g.at[there, rows], s_w.at[w], r_w.at[k, way, step], expert=to)
                elif step == 8 - way:
                    here = step if way == 0 else 16 - step
                    wait(g.at[here, rows], r_w.at[k, way, step - 1])
        if step == 3:
            hand_on(1, 3)
            hand_on(13, 3)
        if step == 6:
            hand_on(4, 3)
            hand_on(10, 3)
        if step == 8:
            hand_on(7, 3)

    @pl.when(core == 1)
    def _():
        ring(0, 0)

    far_half = pl.ds(pl.multiple_of(2304 * (1 - yh), 128), 2304)
    sends.append(
        send(patches.at[0, :, far_half], pv.at[yh], s_one.at[0], r_one.at[0], expert=far, tensor=across)
    )

    def regroup():
        for i in range(1, 4):
            xx = lax.rem(x + i, 4)
            for k, source in enumerate((gate, up)):
                dst = wgu.at[x, :, :, pl.ds(128 * k, 128)]
                send(source.at[:, xx], dst, s_gu, r_gu, tensor=yl * 4 + xx)
        drains.append((wgu.at[pl.ds(0, 3)], s_gu))
        cols = pl.ds(pl.multiple_of((1 - yh) * 2048 + x * 512 + (1 - yl) * 256, 128), 256)
        sends.append(
            send(text.at[0, :, cols], tx.at[yh], s_one.at[1], r_one.at[1], expert=far, tensor=across)
        )

    def iota(shape, dim):
        return lax.broadcasted_iota(I32, shape, dim)

    def route():
        line = iota((32, 128), 0)
        dist = jnp.zeros((32, 128), I32)
        for p, d in enumerate(DISTANCES):
            dist = jnp.where((line >> 1) == p, d, dist)
        expert = (line & 1) * 16 + ((z + dist) & 15)
        member = jnp.zeros((32, 128), F32)
        share = jnp.zeros((32, 128), F32)
        for k in range(8):
            named = ids[k : k + 1, :] == expert
            member = jnp.where(named, 1.0, member)
            share = share + jnp.where(named, shares[k : k + 1, :], 0.0)
        before = (iota((128, 128), 0) < iota((128, 128), 1)).astype(F32).astype(BF)
        rank = nn(member.astype(BF), before)
        swap_own[256:288] = jnp.where(member > 0.5, rank, -1.0).astype(BF)
        wt[...] = share

    def images():
        unit_row = units[...].astype(F32)
        first = (iota((32, 32), 0) < iota((32, 32), 1)).astype(F32).astype(BF)
        starts = nn(jnp.broadcast_to(unit_row, (8, 32)).astype(BF), first)[:1]
        slot = iota((128, 32), 0)
        owner = ((slot >> 1) & 1) * 16 + ((z + (slot >> 3)) & 15)
        match = (owners[...] == owner) & (((slot >> 2) & 1) == yh)

        def pick_out(row):
            return jnp.sum(jnp.where(match, row, 0.0), axis=1, keepdims=True)

        start, count = pick_out(starts), pick_out(unit_row)
        offset = pick_out(offsets[...].astype(F32))
        column = iota((128, 1), 0)
        turn = (column & 1).astype(F32)
        valid = turn < count
        base = (yh * 64).astype(F32)
        source = jnp.where(valid, base + start + turn, -1.0)
        position = jnp.where(valid, ((column >> 1) & 1).astype(F32) * 128.0 + offset + turn, -1.0)
        swap_own[:128] = (iota((128, 128), 1).astype(F32) == source).astype(F32).astype(BF)
        swap_own[128:256] = jnp.broadcast_to(position, (128, 128)).astype(BF)
        sends.append(send(swap_own, swap_far, s_one.at[2], r_one.at[2], expert=far, tensor=across))

    def norm_patches(own, p):
        g = yh if own else 1 - yh
        if p == 0:
            if own:
                local[0].wait()
            else:
                wait(pv.at[g], r_one.at[0])
        part = pl.ds(1152 * p, 1152)
        v = pv[g, :, part].astype(F32)
        center = v - jnp.mean(v, axis=1, keepdims=True)
        variance = jnp.mean(center * center, axis=1, keepdims=True)
        scaled = center * lax.rsqrt(variance + 1e-06) * pgain[...].reshape(1, 1152) + pbias[...].reshape(1, 1152)
        for o in range(8):
            xz[8 * p + o, g] = scaled[:, 144 * o : 144 * o + 144].astype(BF)

    def selections():
        wait(swap_far, r_one.at[2])
        for oy, swap in ((yh, swap_own), (1 - yh, swap_far)):
            ranks = swap[256:288].astype(F32).reshape(32, 1, 128)
            slots = iota((32, 16, 128), 1).astype(F32)
            pick[oy] = (ranks == slots).astype(F32).reshape(512, 128).astype(BF)
        positions = jnp.maximum(swap_own[128:256].astype(F32), swap_far[128:256].astype(F32))
        info_s[...] = positions.reshape(16, 8, 128)

    jobs = {
        0: [regroup, route],
        1: [images],
        2: [lambda: norm_patches(True, 0)],
        3: [lambda: norm_patches(True, 1)],
        4: [selections],
        5: [lambda: norm_patches(False, 0)],
        6: [lambda: norm_patches(False, 1)],
    }
    for s in range(8):

        @pl.when(core == 1)
        def _():
            ring(0, s + 1)
            if s + 1 >= 2:
                ring(1, s + 1 - 2)

        for job in jobs.get(s, ()):
            job()

    @pl.when(core == 0)
    def _():
        wait(g1.at[pl.ds(1, 15)], r_c.at[0])

    w1x[...] = jnp.zeros((16, 144, 128), BF)
    for r in range(9):
        low = 144 if r < 8 else 160
        w1x[:, 16 * r : 16 * r + 16, :32] = g1[:, low : low + 16, 32 * (r % 8) : 32 * (r % 8) + 32]
    main, tail = jnp.zeros((128, 256), F32), jnp.zeros((128, 128), F32)
    for r in range(16):
        rows = xz[lax.rem(z - r + 16, 16)].reshape(128, 144)
        main = main + nn(rows, g1[r, :144, :])
        tail = tail + nn(rows, w1x[r])
    p1s[:128] = main.astype(BF)
    for r in range(8):
        p1s[128:144, 32 * r : 32 * r + 32] = tail[16 * r : 16 * r + 16, :32].astype(BF)
    sends.append(send(p1s, p1r, s_one.at[3], r_one.at[3], expert=far))

    @pl.when(core == 1)
    def _():
        ring(1, 7)
        ring(1, 8)

    def tell(first, last):
        for d in range(first, last):
            send(info_s.at[d], info_r.at[d], s_info, r_info, expert=yh * 16 + lax.rem(z + d, 16))

    tell(1, 8)

    @pl.when(core == 0)
    def _():
        wait(g2.at[pl.ds(1, 15)], r_c.at[1])

    chosen = swap_own[:128] + swap_far[:128]

    bias = b1[...].reshape(1, 288)

    def gelu(v):
        return (0.5 * v * (1.0 + lax.erf(v * (0.5**0.5)))).astype(BF)

    wait(p1r, r_one.at[3])
    hid[:, :256] = gelu(main + p1r[:128].astype(F32) + bias[:, :256])
    for r in range(8):
        far_tail = p1r[128:144, 32 * r : 32 * r + 32].astype(F32)
        hid[16 * r : 16 * r + 16, 256:] = gelu(tail[16 * r : 16 * r + 16, :32] + far_tail + bias[:, 256:])

    def second(tt):
        k = 2 * lax.rem(tt, 4) + tt // 4
        units_here = hid[...]
        return jnp.concatenate([nn(units_here, g2[lax.rem(z - 2 * k + 16, 16)]), nn(units_here, g2[lax.rem(z - 2 * k + 15, 16)])], axis=1)

    for i in range(1, 8):
        tt = lax.rem(t + i, 8)
        p2s[i - 1] = second(tt).astype(BF)
        send(p2s.at[i - 1], p2r.at[i - 1], s_p2, r_p2, tensor=tt)
    drains.append((p2r.at[pl.ds(0, 7)], s_p2))
    tell(8, 16)
    info_r[0] = info_s[0]
    drains.append((info_r.at[pl.ds(0, 15)], s_info))
    total = second(t) + b2[:, pl.ds(pl.multiple_of(col, 128), 256)]
    wait(p2r.at[pl.ds(0, 7)], r_p2)
    for i in range(7):
        total = total + p2r[i].astype(F32)
    emb = total.astype(BF)

    rows = nn(chosen, emb).reshape(16, 8, 256)
    img_s[...] = jnp.concatenate([rows[:, :, :128], rows[:, :, 128:]], axis=1).astype(BF)
    img_r[0] = img_s[0]
    for d in sorted(range(1, 16), key=lambda d: abs(d - 8)):
        send(img_s.at[d], img_r.at[d], s_img, r_img, expert=yh * 16 + lax.rem(z + d, 16))

    drains.append((img_r.at[pl.ds(0, 15)], s_img))
    local[1].wait()
    wait(tx.at[1 - yh], r_one.at[1])
    wait(info_r.at[pl.ds(0, 15)], r_info)
    position = info_r[...]
    blank = jnp.zeros((16, 8, 128), F32)
    placed = []
    for oy in range(2):
        hit = (position == (iota((16, 8, 128), 2) + oy * 128).astype(F32)).astype(F32)
        low = jnp.concatenate([hit, blank], axis=1).reshape(256, 128).astype(BF)
        high = jnp.concatenate([blank, hit], axis=1).reshape(256, 128).astype(BF)
        covered = tn(low, jnp.ones((256, 128), BF)) > 0.5
        placed.append((low, high, covered))
    wait(img_r.at[pl.ds(0, 15)], r_img)
    arrived = img_r[...].reshape(256, 128)
    for oy in range(2):
        low, high, covered = placed[oy]
        for half, hits in enumerate((low, high)):
            part = pl.ds(128 * half, 128)
            base = tx[oy, :, part].astype(F32)
            st[oy, :, part] = jnp.where(covered, tn(hits, arrived), base).astype(BF)

    for oy in range(2):
        xs[:, :, 16 * oy : 16 * oy + 16, :] = nn(pick[oy], st[oy]).astype(BF).reshape(16, 2, 16, 256)
    for p in range(MOVED):
        if p != HERE:
            send(xs.at[p], xr.at[p], s_disp, r_disp.at[p], expert=yh * 16 + lax.rem(z + DISTANCES[p], 16))
    for p in range(MOVED, 16):
        place = p + PER * (1 - core)
        to = yh * 16 + lax.rem(z + DISTANCES[p], 16)
        send(xs.at[p], xr.at[place], s_disp, r_disp.at[place], expert=to, dp=1)

    drains.append((xr.at[pl.ds(0, 15)], s_disp))

    def forward(c):
        part = pl.ds(PER * c, PER)
        for p in range(PER * c, PER * c + PER):
            if p == HERE:
                xr[p] = xs[p]
            else:
                wait(xr.at[p], r_disp.at[p])
        dst = xk.at[part, y]
        send(xr.at[part, 1 - yh], dst, s_ag, r_ag.at[c], expert=far)
        send(xr.at[part, 1 - yh], dst, s_ag, r_ag.at[c], expert=far, tensor=across)
        send(xr.at[part, yh], dst, s_ag, r_ag.at[c], tensor=across)
        xk[part, y] = xr[part, yh]

    def project(c):
        wait(xk.at[pl.ds(PER * c, PER), pl.ds(0, 3)], r_ag.at[c])
        if c == 0:
            for copy in local[3:]:
                copy.wait()
            wait(wgu.at[pl.ds(0, 3)], r_gu)
        squares = jnp.zeros((8, ROWS), F32)
        ones = jnp.ones((8, 256), BF)
        for yy in range(4):
            v = xk[PER * c : PER * c + PER, yy].reshape(ROWS, 256).astype(F32)
            start = 2048 * (yy // 2) + 256 * (yy % 2) + 512 * x
            gain = tgain[:, pl.ds(pl.multiple_of(start, 128), 256)]
            gx[:, 256 * yy : 256 * yy + 256] = (v * gain).astype(BF)
            square = v * v
            high = square.astype(BF)
            low = (square - high.astype(F32)).astype(BF)
            squares = squares + nt(ones, high) + nt(ones, low)
        ss[c] = squares
        high = squares.astype(BF).astype(F32)
        squares = jnp.concatenate([high, squares - high], axis=0).astype(BF)
        for i in range(1, 4):
            xx = lax.rem(x + i, 4)
            ps[c, i, :ROWS] = nn(gx[...], wgu[xx].reshape(1024, 256)).astype(BF)
            ps[c, i, ROWS:, :ROWS] = squares
            send(ps.at[c, i], pr.at[c, i - 1], s_rs, r_rs.at[c], tensor=yl * 4 + xx)
        ps[c, 0, :ROWS] = nn(gx[...], wgu[x].reshape(1024, 256)).astype(BF)

    def activate(c):
        wait(pr.at[c], r_rs.at[c])
        squares = ss[c, 0:1]
        sums = ps[c, 0, :ROWS].astype(F32)
        for i in range(3):
            both = pr[c, i, ROWS:, :ROWS].astype(F32)
            squares = squares + both[0:1] + both[8:9]
            sums = sums + pr[c, i, :ROWS].astype(F32)
        inverse = lax.rsqrt(squares * (1.0 / 4096.0) + 1e-06)
        eye = iota((ROWS, ROWS), 0) == iota((ROWS, ROWS), 1)
        inverse = jnp.sum(jnp.where(eye, inverse, 0.0), axis=1, keepdims=True)
        sums = sums * inverse
        gated, upped = sums[:, :128], sums[:, 128:]
        activation = (gated / (1.0 + jnp.exp(-gated)) * upped).astype(BF)
        act_s[c] = activation
        mine = pl.ds(pl.multiple_of(t * 128, 128), 128)
        act_r[c, :, mine] = activation
        for i in range(1, 8):
            send(act_s.at[c], act_r.at[c, :, mine], s_act, r_act.at[c], tensor=lax.rem(t + i, 8))

    def produce(c):
        if c == 0:
            local[2].wait()
        wait(act_r.at[c, :, pl.ds(0, 896)], r_act.at[c])
        ob[PER * c : PER * c + PER] = nn(act_r[c], dw[...]).astype(BF).reshape(PER, 2, 16, 512)
        for p in range(PER * c, PER * c + PER):
            home = p - PER if c == CHUNKS else p
            zz = lax.rem(z - DISTANCES[home] + 16, 16)
            dst = rb.at[2 * home + yh]
            if p == HERE:
                rb[2 * p + yh] = ob[p, yh]
                send(ob.at[p, 1 - yh], dst, s_ret, r_ret, expert=far)
            else:
                for oy in range(2):
                    if c == CHUNKS:
                        send(ob.at[p, oy], dst, s_moved, r_ret, expert=oy * 16 + zz, dp=0)
                    else:
                        send(ob.at[p, oy], dst, s_ret, r_ret, expert=oy * 16 + zz)

    def on_turn(step, c):
        if 0 <= c < FULL:
            step(c)
        elif FULL <= c < PARTS:

            @pl.when(core == 1)
            def _():
                step(c)

    for turn in range(PARTS + 3):
        on_turn(forward, turn)
        on_turn(project, turn - 1)
        on_turn(activate, turn - 2)
        on_turn(produce, turn - 3)

    for count, parts in ((2 * MOVED - 1, FULL), (31, PARTS)):

        @pl.when(core == (1 if parts == PARTS else 0))
        def _(count=count, parts=parts):
            wait(xk.at[pl.ds(0, PER * parts), pl.ds(0, 3)], s_ag)
            wait(pr.at[pl.ds(0, parts)], s_rs)
            wait(act_r.at[pl.ds(0, parts), :, pl.ds(0, 896)], s_act)
            wait(rb.at[pl.ds(0, count)], s_ret)
            if parts == PARTS:
                wait(ob.at[pl.ds(16, PER)], s_moved)

    weight = pick[yh].astype(F32).reshape(32, 16, 128) * wt[...].reshape(32, 1, 128)
    weight = weight.reshape(512, 128)
    high = weight.astype(BF)
    low = (weight - high.astype(F32)).astype(BF)
    wait(rb.at[pl.ds(0, 31)], r_ret)
    back = rb[...].reshape(512, 512)
    out[0] = (tn(high, back) + tn(low, back)).astype(BF)

    finish()


def body(
    patches, patch_gain, patch_bias, first_weight, first_bias, second_weight, second_bias,
    image_units, image_owner, image_offset, text_states, token_gain, expert_ids,
    route_weights, gate_weight, up_weight, down_weight,
):
    vmem = pl.BlockSpec(memory_space=pltpu.VMEM)
    hbm = pl.BlockSpec(memory_space=pltpu.HBM)
    dma = pltpu.SemaphoreType.DMA
    scratch = [
        pltpu.VMEM((16, 176, 256), BF),
        pltpu.VMEM((16, 288, 128), BF),
        pltpu.VMEM((16, 144, 128), BF),
        pltpu.VMEM((2, 64, 2304), BF),
        pltpu.VMEM((16, 2, 64, 144), BF),
        pltpu.VMEM((128, 288), BF),
        pltpu.VMEM((144, 256), BF),
        pltpu.VMEM((144, 256), BF),
        pltpu.VMEM((7, 128, 256), BF),
        pltpu.VMEM((7, 128, 256), BF),
        pltpu.VMEM((288, 128), BF),
        pltpu.VMEM((288, 128), BF),
        pltpu.VMEM((16, 8, 128), F32),
        pltpu.VMEM((16, 8, 128), F32),
        pltpu.VMEM((16, 16, 128), BF),
        pltpu.VMEM((16, 16, 128), BF),
        pltpu.VMEM((2, 128, 256), BF),
        pltpu.VMEM((32, 128), F32),
        pltpu.VMEM((2, 512, 128), BF),
        pltpu.VMEM((2, 128, 256), BF),
        pltpu.VMEM((16, 2, 32, 256), BF),
        pltpu.VMEM((16 + PER, 2, 32, 256), BF),
        pltpu.VMEM((16 + PER, 4, 32, 256), BF),
        pltpu.VMEM((4, 2, 512, 256), BF),
        pltpu.VMEM((1024, 512), BF),
        pltpu.VMEM((ROWS, 1024), BF),
        pltpu.VMEM((PARTS, 4, ROWS + 16, 256), BF),
        pltpu.VMEM((PARTS, 3, ROWS + 16, 256), BF),
        pltpu.VMEM((PARTS, 8, ROWS), F32),
        pltpu.VMEM((PARTS, ROWS, 128), BF),
        pltpu.VMEM((PARTS, ROWS, 1024), BF),
        pltpu.VMEM((16 + PER, 2, 16, 512), BF),
        pltpu.VMEM((32, 16, 512), BF),
        dma((2,)), dma((3, 2, 8)), dma((2,)), dma((2,)),
        dma((5,)), dma, dma, dma((4,)), dma((4,)),
        dma, dma, dma, dma, dma, dma,
        dma, dma((16 + PER,)), dma, dma((PARTS,)),
        dma, dma((PARTS,)), dma, dma((PARTS,)),
        dma, dma, dma,
    ]
    call = pl.pallas_call(
        kernel,
        out_shape=jax.ShapeDtypeStruct((1, 128, 512), BF),
        in_specs=[
            hbm, vmem, vmem, vmem, vmem, vmem, vmem, vmem, vmem, vmem, hbm, vmem,
            vmem, vmem, hbm, hbm, hbm,
        ],
        out_specs=vmem,
        scratch_shapes=scratch,
        compiler_params=pltpu.CompilerParams(
            collective_id=0, has_side_effects=True, vmem_limit_bytes=60 * 1024 * 1024
        ),
    )
    return call(
        patches, patch_gain, patch_bias, first_weight, first_bias,
        second_weight.T, second_bias[None], image_units, image_owner, image_offset,
        text_states, token_gain[None], expert_ids[0].T, route_weights[0].T,
        gate_weight.reshape(2, 4, 512, 128), up_weight.reshape(2, 4, 512, 128), down_weight,
    )


def solution(mesh):
    in_specs = (
        P(("dp", "expert"), None, None),
        P(),
        P(),
        P("expert", "tensor"),
        P("tensor"),
        P("expert", "tensor"),
        P(),
        P(("dp", "expert"), None),
        P(("dp", "expert"), None),
        P(("dp", "expert"), None),
        P(("dp", "expert"), None, None),
        P(),
        P(("dp", "expert"), None, None),
        P(("dp", "expert"), None, None),
        P("expert", None, "tensor"),
        P("expert", None, "tensor"),
        P("expert", None, "tensor"),
    )
    out_specs = P(("dp", "expert"), None, "tensor")
    return jax.shard_map(body, mesh=mesh, in_specs=in_specs, out_specs=out_specs, check_vma=False)
```

```python
import jax
import jax.numpy as jnp
from jax import lax
from jax.experimental import pallas as pl
from jax.experimental.pallas import tpu as pltpu
from jax.sharding import PartitionSpec as P

BF = jnp.bfloat16
F32 = jnp.float32
I32 = jnp.int32
MESH = pl.DeviceIdType.MESH

PLANES = 16
CHUNKS = 8
PER = PLANES // CHUNKS
ROWS = PER * 32
PARTS = CHUNKS + 1
FULL = CHUNKS - 1
MOVED = PER * FULL


DISTANCES = (0, 8, 1, 15, 7, 9, 2, 14, 6, 10, 3, 13, 5, 11, 4, 12)
HERE = DISTANCES.index(0)


def nn(a, b):
    return jnp.dot(a, b, preferred_element_type=F32)


def nt(a, b):
    return lax.dot_general(a, b, (((1,), (1,)), ((), ())), preferred_element_type=F32)


def tn(a, b):
    return lax.dot_general(a, b, (((0,), (0,)), ((), ())), preferred_element_type=F32)


def wait(ref, sem):
    pltpu.make_async_copy(ref, ref, sem).wait()


def kernel(
    patches, pgain, pbias, w1, b1, w2, b2, units, owners, offsets, text, tgain,
    ids, shares, gate, up, down,
    out,
    g1, g2, w1x, pv, xz, hid, p1s, p1r, p2s, p2r, swap_own, swap_far, info_s, info_r,
    img_s, img_r, tx, wt, pick, st, xs, xr, xk, wgu, dw, gx, ps, pr, ss, act_s, act_r, ob, rb,
    s_w, r_w, s_c, r_c, l_sem, s_gu, r_gu, s_one, r_one, s_info, r_info, s_p2, r_p2,
    s_img, r_img, s_disp, r_disp, s_ag, r_ag, s_rs, r_rs, s_act, r_act,
    s_ret, r_ret, s_moved,
):
    e = lax.axis_index("expert")
    t = lax.axis_index("tensor")
    core = lax.axis_index("dp")
    yh, z = e // 16, e % 16
    yl, x = t // 4, t % 4
    y = 2 * yh + yl
    far = (1 - yh) * 16 + z
    col = yh * 2048 + x * 512 + yl * 256

    def send(src, dst, ssem, rsem, **dev):
        copy = pltpu.make_async_remote_copy(
            src_ref=src, dst_ref=dst, send_sem=ssem, recv_sem=rsem,
            device_id=dev, device_id_type=MESH,
        )
        copy.start()
        return copy

    local = [
        (patches.at[0, :, pl.ds(pl.multiple_of(2304 * yh, 128), 2304)], pv.at[yh]),
        (text.at[0, :, pl.ds(pl.multiple_of(col, 128), 256)], tx.at[yh]),
        (down.at[0], dw),
    ]
    for k, source in enumerate((gate, up)):
        local.append((source.at[:, x], wgu.at[x, :, :, pl.ds(128 * k, 128)]))
    local = [pltpu.make_async_copy(a, b, l_sem.at[i]) for i, (a, b) in enumerate(local)]
    barrier = pltpu.get_barrier_semaphore()
    after = yh * 16 + lax.rem(z + 1, 16)
    ahead = yh * 16 + lax.rem(z + 15, 16)
    across = lax.rem(t + 4, 8)

    def greet(**dev):
        pl.semaphore_signal(barrier, inc=1, device_id=dev, device_id_type=MESH)

    greet(expert=after)
    greet(expert=ahead)
    greet(dp=1 - core)
    for i in range(1, 8):
        greet(tensor=lax.rem(t + i, 8))
    greet(expert=far)
    greet(expert=far, tensor=across)

    for copy in local:
        copy.start()

    g1[0, :144, :] = w1[:, :256]
    for r in range(9):
        low = 144 if r < 8 else 160
        g1[0, low : low + 16, 32 * (r % 8) : 32 * (r % 8) + 32] = w1[16 * r : 16 * r + 16, 256:288]
    g2[0] = w2[...]

    pl.semaphore_wait(barrier, 12)

    sends, drains = [], []

    def finish():
        for copy in sends:
            copy.wait_send()
        for ref, sem in drains:
            wait(ref, sem)

        for w, g in enumerate(gathered):

            @pl.when(core == 1)
            def _(w=w, g=g):
                wait(g.at[pl.ds(1, 15)], s_w.at[w])
                wait(g.at[pl.ds(1, 15)], s_c.at[w])

    gathered = (g1, g2)
    pieces = (((0, 0, 96), (1, 96, 80)), ((2, 0, 288),))

    def ring(w, step):
        g = gathered[w]

        def hand_on(first, count):
            blocks = g.at[pl.ds(first, count)]
            send(blocks, blocks, s_c.at[w], r_c.at[w], dp=0)

        for k, low, size in pieces[w]:
            rows = pl.ds(low, size)
            for way, to in enumerate((after, ahead)):
                if step < 8 - way:
                    here, there = (step, step + 1) if way == 0 else ((16 - step) % 16, 15 - step)
                    if step > 0:
                        wait(g.at[here, rows], r_w.at[k, way, step - 1])
                    send(g.at[here, rows], g.at[there, rows], s_w.at[w], r_w.at[k, way, step], expert=to)
                elif step == 8 - way:
                    here = step if way == 0 else 16 - step
                    wait(g.at[here, rows], r_w.at[k, way, step - 1])
        if step == 4:
            hand_on(1, 4)
            hand_on(12, 4)
        if step == 7:
            hand_on(5, 3)
            hand_on(9, 3)
        if step == 8:
            hand_on(8, 1)

    @pl.when(core == 1)
    def _():
        ring(0, 0)

    far_half = pl.ds(pl.multiple_of(2304 * (1 - yh), 128), 2304)
    sends.append(
        send(patches.at[0, :, far_half], pv.at[yh], s_one.at[0], r_one.at[0], expert=far, tensor=across)
    )

    def regroup():
        for i in range(1, 4):
            xx = lax.rem(x + i, 4)
            for k, source in enumerate((gate, up)):
                dst = wgu.at[x, :, :, pl.ds(128 * k, 128)]
                send(source.at[:, xx], dst, s_gu, r_gu, tensor=yl * 4 + xx)
        drains.append((wgu.at[pl.ds(0, 3)], s_gu))
        cols = pl.ds(pl.multiple_of((1 - yh) * 2048 + x * 512 + (1 - yl) * 256, 128), 256)
        sends.append(
            send(text.at[0, :, cols], tx.at[yh], s_one.at[1], r_one.at[1], expert=far, tensor=across)
        )

    def iota(shape, dim):
        return lax.broadcasted_iota(I32, shape, dim)

    def route():
        line = iota((32, 128), 0)
        dist = jnp.zeros((32, 128), I32)
        for p, d in enumerate(DISTANCES):
            dist = jnp.where((line >> 1) == p, d, dist)
        expert = (line & 1) * 16 + ((z + dist) & 15)
        member = jnp.zeros((32, 128), F32)
        share = jnp.zeros((32, 128), F32)
        for k in range(8):
            named = ids[k : k + 1, :] == expert
            member = jnp.where(named, 1.0, member)
            share = share + jnp.where(named, shares[k : k + 1, :], 0.0)
        before = (iota((128, 128), 0) < iota((128, 128), 1)).astype(F32).astype(BF)
        rank = nn(member.astype(BF), before)
        swap_own[256:288] = jnp.where(member > 0.5, rank, -1.0).astype(BF)
        wt[...] = share

    def images():
        unit_row = units[...].astype(F32)
        first = (iota((32, 32), 0) < iota((32, 32), 1)).astype(F32).astype(BF)
        starts = nn(jnp.broadcast_to(unit_row, (8, 32)).astype(BF), first)[:1]
        slot = iota((128, 32), 0)
        owner = ((slot >> 1) & 1) * 16 + ((z + (slot >> 3)) & 15)
        match = (owners[...] == owner) & (((slot >> 2) & 1) == yh)

        def pick_out(row):
            return jnp.sum(jnp.where(match, row, 0.0), axis=1, keepdims=True)

        start, count = pick_out(starts), pick_out(unit_row)
        offset = pick_out(offsets[...].astype(F32))
        column = iota((128, 1), 0)
        turn = (column & 1).astype(F32)
        valid = turn < count
        base = (yh * 64).astype(F32)
        source = jnp.where(valid, base + start + turn, -1.0)
        position = jnp.where(valid, ((column >> 1) & 1).astype(F32) * 128.0 + offset + turn, -1.0)
        swap_own[:128] = (iota((128, 128), 1).astype(F32) == source).astype(F32).astype(BF)
        swap_own[128:256] = jnp.broadcast_to(position, (128, 128)).astype(BF)
        sends.append(send(swap_own, swap_far, s_one.at[2], r_one.at[2], expert=far, tensor=across))

    def norm_patches(own, p):
        g = yh if own else 1 - yh
        if p == 0:
            if own:
                local[0].wait()
            else:
                wait(pv.at[g], r_one.at[0])
        part = pl.ds(1152 * p, 1152)
        v = pv[g, :, part].astype(F32)
        center = v - jnp.mean(v, axis=1, keepdims=True)
        variance = jnp.mean(center * center, axis=1, keepdims=True)
        scaled = center * lax.rsqrt(variance + 1e-06) * pgain[...].reshape(1, 1152) + pbias[...].reshape(1, 1152)
        for o in range(8):
            xz[8 * p + o, g] = scaled[:, 144 * o : 144 * o + 144].astype(BF)

    def selections():
        wait(swap_far, r_one.at[2])
        for oy, swap in ((yh, swap_own), (1 - yh, swap_far)):
            ranks = swap[256:288].astype(F32).reshape(32, 1, 128)
            slots = iota((32, 16, 128), 1).astype(F32)
            pick[oy] = (ranks == slots).astype(F32).reshape(512, 128).astype(BF)
        positions = jnp.maximum(swap_own[128:256].astype(F32), swap_far[128:256].astype(F32))
        info_s[...] = positions.reshape(16, 8, 128)

    jobs = {
        0: [regroup, route],
        1: [images],
        2: [lambda: norm_patches(True, 0)],
        3: [lambda: norm_patches(True, 1)],
        4: [selections],
        5: [lambda: norm_patches(False, 0)],
        6: [lambda: norm_patches(False, 1)],
    }
    for s in range(8):

        @pl.when(core == 1)
        def _():
            ring(0, s + 1)
            if s + 1 >= 2:
                ring(1, s + 1 - 2)

        for job in jobs.get(s, ()):
            job()

    @pl.when(core == 0)
    def _():
        wait(g1.at[pl.ds(1, 15)], r_c.at[0])

    w1x[...] = jnp.zeros((16, 144, 128), BF)
    for r in range(9):
        low = 144 if r < 8 else 160
        w1x[:, 16 * r : 16 * r + 16, :32] = g1[:, low : low + 16, 32 * (r % 8) : 32 * (r % 8) + 32]
    main, tail = jnp.zeros((128, 256), F32), jnp.zeros((128, 128), F32)
    for r in range(16):
        rows = xz[lax.rem(z - r + 16, 16)].reshape(128, 144)
        main = main + nn(rows, g1[r, :144, :])
        tail = tail + nn(rows, w1x[r])
    p1s[:128] = main.astype(BF)
    for r in range(8):
        p1s[128:144, 32 * r : 32 * r + 32] = tail[16 * r : 16 * r + 16, :32].astype(BF)
    sends.append(send(p1s, p1r, s_one.at[3], r_one.at[3], expert=far))

    @pl.when(core == 1)
    def _():
        ring(1, 7)
        ring(1, 8)

    def tell(first, last):
        for d in range(first, last):
            send(info_s.at[d], info_r.at[d], s_info, r_info, expert=yh * 16 + lax.rem(z + d, 16))

    tell(1, 8)

    @pl.when(core == 0)
    def _():
        wait(g2.at[pl.ds(1, 15)], r_c.at[1])

    chosen = swap_own[:128] + swap_far[:128]

    bias = b1[...].reshape(1, 288)

    def gelu(v):
        return (0.5 * v * (1.0 + lax.erf(v * (0.5**0.5)))).astype(BF)

    wait(p1r, r_one.at[3])
    hid[:, :256] = gelu(main + p1r[:128].astype(F32) + bias[:, :256])
    for r in range(8):
        far_tail = p1r[128:144, 32 * r : 32 * r + 32].astype(F32)
        hid[16 * r : 16 * r + 16, 256:] = gelu(tail[16 * r : 16 * r + 16, :32] + far_tail + bias[:, 256:])

    def second(tt):
        k = 2 * lax.rem(tt, 4) + tt // 4
        units_here = hid[...]
        return jnp.concatenate([nn(units_here, g2[lax.rem(z - 2 * k + 16, 16)]), nn(units_here, g2[lax.rem(z - 2 * k + 15, 16)])], axis=1)

    for i in range(1, 8):
        tt = lax.rem(t + i, 8)
        p2s[i - 1] = second(tt).astype(BF)
        send(p2s.at[i - 1], p2r.at[i - 1], s_p2, r_p2, tensor=tt)
    drains.append((p2r.at[pl.ds(0, 7)], s_p2))
    tell(8, 16)
    info_r[0] = info_s[0]
    drains.append((info_r.at[pl.ds(0, 15)], s_info))
    total = second(t) + b2[:, pl.ds(pl.multiple_of(col, 128), 256)]
    wait(p2r.at[pl.ds(0, 7)], r_p2)
    for i in range(7):
        total = total + p2r[i].astype(F32)
    emb = total.astype(BF)

    rows = nn(chosen, emb).reshape(16, 8, 256)
    img_s[...] = jnp.concatenate([rows[:, :, :128], rows[:, :, 128:]], axis=1).astype(BF)
    img_r[0] = img_s[0]
    for d in sorted(range(1, 16), key=lambda d: abs(d - 8)):
        send(img_s.at[d], img_r.at[d], s_img, r_img, expert=yh * 16 + lax.rem(z + d, 16))

    drains.append((img_r.at[pl.ds(0, 15)], s_img))
    local[1].wait()
    wait(tx.at[1 - yh], r_one.at[1])
    wait(info_r.at[pl.ds(0, 15)], r_info)
    position = info_r[...]
    blank = jnp.zeros((16, 8, 128), F32)
    placed = []
    for oy in range(2):
        hit = (position == (iota((16, 8, 128), 2) + oy * 128).astype(F32)).astype(F32)
        low = jnp.concatenate([hit, blank], axis=1).reshape(256, 128).astype(BF)
        high = jnp.concatenate([blank, hit], axis=1).reshape(256, 128).astype(BF)
        covered = tn(low, jnp.ones((256, 128), BF)) > 0.5
        placed.append((low, high, covered))
    wait(img_r.at[pl.ds(0, 15)], r_img)
    arrived = img_r[...].reshape(256, 128)
    for oy in range(2):
        low, high, covered = placed[oy]
        for half, hits in enumerate((low, high)):
            part = pl.ds(128 * half, 128)
            base = tx[oy, :, part].astype(F32)
            st[oy, :, part] = jnp.where(covered, tn(hits, arrived), base).astype(BF)

    for oy in range(2):
        xs[:, :, 16 * oy : 16 * oy + 16, :] = nn(pick[oy], st[oy]).astype(BF).reshape(16, 2, 16, 256)
    for p in range(MOVED):
        if p != HERE:
            send(xs.at[p], xr.at[p], s_disp, r_disp.at[p], expert=yh * 16 + lax.rem(z + DISTANCES[p], 16))
    for p in range(MOVED, 16):
        place = p + PER * (1 - core)
        to = yh * 16 + lax.rem(z + DISTANCES[p], 16)
        send(xs.at[p], xr.at[place], s_disp, r_disp.at[place], expert=to, dp=1)

    drains.append((xr.at[pl.ds(0, 15)], s_disp))

    def forward(c):
        part = pl.ds(PER * c, PER)
        for p in range(PER * c, PER * c + PER):
            if p == HERE:
                xr[p] = xs[p]
            else:
                wait(xr.at[p], r_disp.at[p])
        dst = xk.at[part, y]
        send(xr.at[part, 1 - yh], dst, s_ag, r_ag.at[c], expert=far)
        send(xr.at[part, 1 - yh], dst, s_ag, r_ag.at[c], expert=far, tensor=across)
        send(xr.at[part, yh], dst, s_ag, r_ag.at[c], tensor=across)
        xk[part, y] = xr[part, yh]

    def project(c):
        wait(xk.at[pl.ds(PER * c, PER), pl.ds(0, 3)], r_ag.at[c])
        if c == 0:
            for copy in local[3:]:
                copy.wait()
            wait(wgu.at[pl.ds(0, 3)], r_gu)
        squares = jnp.zeros((8, ROWS), F32)
        ones = jnp.ones((8, 256), BF)
        for yy in range(4):
            v = xk[PER * c : PER * c + PER, yy].reshape(ROWS, 256).astype(F32)
            start = 2048 * (yy // 2) + 256 * (yy % 2) + 512 * x
            gain = tgain[:, pl.ds(pl.multiple_of(start, 128), 256)]
            gx[:, 256 * yy : 256 * yy + 256] = (v * gain).astype(BF)
            square = v * v
            high = square.astype(BF)
            low = (square - high.astype(F32)).astype(BF)
            squares = squares + nt(ones, high) + nt(ones, low)
        ss[c] = squares
        high = squares.astype(BF).astype(F32)
        squares = jnp.concatenate([high, squares - high], axis=0).astype(BF)
        for i in range(1, 4):
            xx = lax.rem(x + i, 4)
            ps[c, i, :ROWS] = nn(gx[...], wgu[xx].reshape(1024, 256)).astype(BF)
            ps[c, i, ROWS:, :ROWS] = squares
            send(ps.at[c, i], pr.at[c, i - 1], s_rs, r_rs.at[c], tensor=yl * 4 + xx)
        ps[c, 0, :ROWS] = nn(gx[...], wgu[x].reshape(1024, 256)).astype(BF)

    def activate(c):
        wait(pr.at[c], r_rs.at[c])
        squares = ss[c, 0:1]
        sums = ps[c, 0, :ROWS].astype(F32)
        for i in range(3):
            both = pr[c, i, ROWS:, :ROWS].astype(F32)
            squares = squares + both[0:1] + both[8:9]
            sums = sums + pr[c, i, :ROWS].astype(F32)
        inverse = lax.rsqrt(squares * (1.0 / 4096.0) + 1e-06)
        eye = iota((ROWS, ROWS), 0) == iota((ROWS, ROWS), 1)
        inverse = jnp.sum(jnp.where(eye, inverse, 0.0), axis=1, keepdims=True)
        sums = sums * inverse
        gated, upped = sums[:, :128], sums[:, 128:]
        activation = (gated / (1.0 + jnp.exp(-gated)) * upped).astype(BF)
        act_s[c] = activation
        mine = pl.ds(pl.multiple_of(t * 128, 128), 128)
        act_r[c, :, mine] = activation
        for i in range(1, 8):
            send(act_s.at[c], act_r.at[c, :, mine], s_act, r_act.at[c], tensor=lax.rem(t + i, 8))

    def produce(c):
        if c == 0:
            local[2].wait()
        wait(act_r.at[c, :, pl.ds(0, 896)], r_act.at[c])
        ob[PER * c : PER * c + PER] = nn(act_r[c], dw[...]).astype(BF).reshape(PER, 2, 16, 512)
        for p in range(PER * c, PER * c + PER):
            home = p - PER if c == CHUNKS else p
            zz = lax.rem(z - DISTANCES[home] + 16, 16)
            dst = rb.at[2 * home + yh]
            if p == HERE:
                rb[2 * p + yh] = ob[p, yh]
                send(ob.at[p, 1 - yh], dst, s_ret, r_ret, expert=far)
            else:
                for oy in range(2):
                    if c == CHUNKS:
                        send(ob.at[p, oy], dst, s_moved, r_ret, expert=oy * 16 + zz, dp=0)
                    else:
                        send(ob.at[p, oy], dst, s_ret, r_ret, expert=oy * 16 + zz)

    def on_turn(step, c):
        if 0 <= c < FULL:
            step(c)
        elif FULL <= c < PARTS:

            @pl.when(core == 1)
            def _():
                step(c)

    for turn in range(PARTS + 3):
        on_turn(forward, turn)
        on_turn(project, turn - 1)
        on_turn(activate, turn - 2)
        on_turn(produce, turn - 3)

    for count, parts in ((2 * MOVED - 1, FULL), (31, PARTS)):

        @pl.when(core == (1 if parts == PARTS else 0))
        def _(count=count, parts=parts):
            wait(xk.at[pl.ds(0, PER * parts), pl.ds(0, 3)], s_ag)
            wait(pr.at[pl.ds(0, parts)], s_rs)
            wait(act_r.at[pl.ds(0, parts), :, pl.ds(0, 896)], s_act)
            wait(rb.at[pl.ds(0, count)], s_ret)
            if parts == PARTS:
                wait(ob.at[pl.ds(16, PER)], s_moved)

    weight = pick[yh].astype(F32).reshape(32, 16, 128) * wt[...].reshape(32, 1, 128)
    weight = weight.reshape(512, 128)
    high = weight.astype(BF)
    low = (weight - high.astype(F32)).astype(BF)
    wait(rb.at[pl.ds(0, 31)], r_ret)
    back = rb[...].reshape(512, 512)
    out[0] = (tn(high, back) + tn(low, back)).astype(BF)

    finish()


def body(
    patches, patch_gain, patch_bias, first_weight, first_bias, second_weight, second_bias,
    image_units, image_owner, image_offset, text_states, token_gain, expert_ids,
    route_weights, gate_weight, up_weight, down_weight,
):
    vmem = pl.BlockSpec(memory_space=pltpu.VMEM)
    hbm = pl.BlockSpec(memory_space=pltpu.HBM)
    dma = pltpu.SemaphoreType.DMA
    scratch = [
        pltpu.VMEM((16, 176, 256), BF),
        pltpu.VMEM((16, 288, 128), BF),
        pltpu.VMEM((16, 144, 128), BF),
        pltpu.VMEM((2, 64, 2304), BF),
        pltpu.VMEM((16, 2, 64, 144), BF),
        pltpu.VMEM((128, 288), BF),
        pltpu.VMEM((144, 256), BF),
        pltpu.VMEM((144, 256), BF),
        pltpu.VMEM((7, 128, 256), BF),
        pltpu.VMEM((7, 128, 256), BF),
        pltpu.VMEM((288, 128), BF),
        pltpu.VMEM((288, 128), BF),
        pltpu.VMEM((16, 8, 128), F32),
        pltpu.VMEM((16, 8, 128), F32),
        pltpu.VMEM((16, 16, 128), BF),
        pltpu.VMEM((16, 16, 128), BF),
        pltpu.VMEM((2, 128, 256), BF),
        pltpu.VMEM((32, 128), F32),
        pltpu.VMEM((2, 512, 128), BF),
        pltpu.VMEM((2, 128, 256), BF),
        pltpu.VMEM((16, 2, 32, 256), BF),
        pltpu.VMEM((16 + PER, 2, 32, 256), BF),
        pltpu.VMEM((16 + PER, 4, 32, 256), BF),
        pltpu.VMEM((4, 2, 512, 256), BF),
        pltpu.VMEM((1024, 512), BF),
        pltpu.VMEM((ROWS, 1024), BF),
        pltpu.VMEM((PARTS, 4, ROWS + 16, 256), BF),
        pltpu.VMEM((PARTS, 3, ROWS + 16, 256), BF),
        pltpu.VMEM((PARTS, 8, ROWS), F32),
        pltpu.VMEM((PARTS, ROWS, 128), BF),
        pltpu.VMEM((PARTS, ROWS, 1024), BF),
        pltpu.VMEM((16 + PER, 2, 16, 512), BF),
        pltpu.VMEM((32, 16, 512), BF),
        dma((2,)), dma((3, 2, 8)), dma((2,)), dma((2,)),
        dma((5,)), dma, dma, dma((4,)), dma((4,)),
        dma, dma, dma, dma, dma, dma,
        dma, dma((16 + PER,)), dma, dma((PARTS,)),
        dma, dma((PARTS,)), dma, dma((PARTS,)),
        dma, dma, dma,
    ]
    call = pl.pallas_call(
        kernel,
        out_shape=jax.ShapeDtypeStruct((1, 128, 512), BF),
        in_specs=[
            hbm, vmem, vmem, vmem, vmem, vmem, vmem, vmem, vmem, vmem, hbm, vmem,
            vmem, vmem, hbm, hbm, hbm,
        ],
        out_specs=vmem,
        scratch_shapes=scratch,
        compiler_params=pltpu.CompilerParams(
            collective_id=0, has_side_effects=True, vmem_limit_bytes=60 * 1024 * 1024
        ),
    )
    return call(
        patches, patch_gain, patch_bias, first_weight, first_bias,
        second_weight.T, second_bias[None], image_units, image_owner, image_offset,
        text_states, token_gain[None], expert_ids[0].T, route_weights[0].T,
        gate_weight.reshape(2, 4, 512, 128), up_weight.reshape(2, 4, 512, 128), down_weight,
    )


def solution(mesh):
    in_specs = (
        P(("dp", "expert"), None, None),
        P(),
        P(),
        P("expert", "tensor"),
        P("tensor"),
        P("expert", "tensor"),
        P(),
        P(("dp", "expert"), None),
        P(("dp", "expert"), None),
        P(("dp", "expert"), None),
        P(("dp", "expert"), None, None),
        P(),
        P(("dp", "expert"), None, None),
        P(("dp", "expert"), None, None),
        P("expert", None, "tensor"),
        P("expert", None, "tensor"),
        P("expert", None, "tensor"),
    )
    out_specs = P(("dp", "expert"), None, "tensor")
    return jax.shard_map(body, mesh=mesh, in_specs=in_specs, out_specs=out_specs, check_vma=False)
```
